256 devices in a mesh: dp: 32 (over z, x), col: 8 (over y, core).
Axes of the slice: x: 4, y: 4, z: 8, core: 2. Of those that a mesh axis runs over, the one named last changes fastest.
Arguments:
- grads: bfloat16 [32, 32768, 512], P('dp', 'col'), may hold values from -8 to 8
- momentum: float32 [32768, 512], P(('col', 'dp')), may hold values from -6 to 6
- weight: float32 [32768, 512], P(('col', 'dp')), may hold values from -0.3125 to 0.3125
- max_logits: int32 [32, 2, 64], P('dp'), may hold values from 0 to 3200, as said below
- threshold: int32 [1], replicated, may hold values from 1200 to 2000
Outputs:
- new_master: float32 [32768, 512], P(('col', 'dp'))
- new_momentum: float32 [32768, 512], P(('col', 'dp'))
- new_weight: bfloat16 [32768, 512], P('col')
- blend_rms: float32 [8], P('col')
The draws below stay inside these ranges and needn't reach their ends.
Inputs may be any that keep to these rules, and one draw needn't show every extreme that they name: `max_logits`: in each layer, every head's largest value over the replicas is held by one replica; each replica holds it for 2 heads. Every value is 400 or more for at least one replica.
All inputs are finite; a program needn't handle non-finite values.
Results may differ from the reference program's by a relative error of at most 0.00045.
Values may be sent and summed in bfloat16 or wider, within the bound.
A program may use at most 64 MiB of HBM per device.

```python
import jax
import jax.numpy as jnp
from jax import lax

R = 512
HEADS = 64
NOPE = 128
VDIM = 128
ITERS = 5
LAYERS = 2
F = 16384
N_DP = 32
N_COL = 8


def layer_logits(key):
    key_order, key_high, key_any, key_other = jax.random.split(key, 4)
    order = jax.random.permutation(key_order, HEADS).astype(jnp.int32)
    owner = order % N_DP
    high_base = jax.random.randint(key_high, (HEADS,), 2400, 3201)
    any_base = jax.random.randint(key_any, (HEADS,), 400, 3201)
    base = jnp.where(order < N_DP, high_base, any_base)
    base = jnp.where(order == 0, 3200, base)
    others = jax.random.randint(key_other, (N_DP, HEADS), 0, base[None, :] // 2 + 1)
    replica = jnp.arange(N_DP, dtype=jnp.int32)[:, None]
    return jnp.where(replica == owner[None, :], base[None, :], others).astype(jnp.int32)


def draw_max_logits(key, part):
    key = jax.random.fold_in(key, 11)
    stacked = [layer_logits(jax.random.fold_in(key, layer)) for layer in range(LAYERS)]
    return jnp.stack(stacked, axis=1).astype(jnp.int32)


def draw_momentum(key, part):
    key = jax.random.fold_in(key, 23)
    total_rows = LAYERS * F
    rows_device = total_rows // (N_COL * N_DP)
    position = (jnp.arange(total_rows, dtype=jnp.int32) // rows_device % N_DP).astype(jnp.float32)
    ramp = position / jnp.float32(N_DP - 1)
    scale = 0.3 * (1.0 + 3.0 * ramp)
    values = jax.random.normal(key, (total_rows, R), jnp.float32)
    return jnp.clip(values * scale[:, None], -6.0, 6.0).astype(jnp.float32)


def draw_grads(key, part):
    key = jax.random.fold_in(key, 31)
    key_noise, key_common, key_scale, key_left, key_right, key_pair = jax.random.split(key, 6)
    total_rows = LAYERS * F
    rows_device = total_rows // (N_COL * N_DP)
    position = jnp.arange(total_rows, dtype=jnp.int32) // rows_device % N_DP
    ramp = position.astype(jnp.float32) / jnp.float32(N_DP - 1)
    pairing = jax.random.permutation(key_pair, N_DP).astype(jnp.int32)
    spike = jnp.where(pairing[:, None] == position[None, :], jnp.float32(3.0), jnp.float32(1.0))
    col_scale = jnp.exp(jax.random.uniform(key_scale, (R,), jnp.float32, -2.0, 2.0))
    left = jax.random.normal(key_left, (total_rows, 4), jnp.float32)
    right = jax.random.normal(key_right, (4, R), jnp.float32)
    low_rank = left[:, 0:1] * right[0:1, :] + left[:, 1:2] * right[1:2, :]
    low_rank = low_rank + left[:, 2:3] * right[2:3, :] + left[:, 3:4] * right[3:4, :]
    noise = jax.random.normal(key_noise, (N_DP, total_rows, R), jnp.float32)
    common_full = jax.random.normal(key_common, (total_rows, R), jnp.float32)
    row_scale = 1.0 + ramp
    full_coef = 0.2
    common = row_scale[:, None] * (full_coef * col_scale[None, :] * common_full + 0.2 * low_rank)
    values = noise * spike[:, :, None] + common[None, :, :]
    return jnp.clip(values, -8.0, 8.0).astype(jnp.bfloat16)


def levels(key, extent, pieces, low, high):
    level, own = 1.0, jax.random.fold_in(key, 6)
    for dim, parts in pieces:
        steps = jnp.exp(jax.random.uniform(jax.random.fold_in(own, dim), (parts,), jnp.float32, low / len(pieces), high / len(pieces)))
        level = level * jnp.repeat(steps, extent[dim] // parts).reshape([-1 if axis == dim else 1 for axis in range(len(extent))])
    return level


def normal_values(rng, extent, spread, most, cuts=(), kind=jnp.bfloat16):
    values = spread * jax.random.normal(rng, extent, jnp.float32)
    if cuts:
        values = values * levels(rng, extent, cuts, -0.22, 0.18)
    return jnp.clip(values, -most, most).astype(kind)


def setup_inputs(seed: int = 0) -> dict:
    key_of = jax.random.split(jax.random.key(seed), 6)
    return {
        "grads": draw_grads(jax.random.fold_in(key_of[5], 71), 0),
        "momentum": draw_momentum(jax.random.fold_in(key_of[5], 71), 0),
        "weight": normal_values(key_of[2], (LAYERS * F, R), 0.02, 0.3125, ((0, 256),), jnp.float32),
        "max_logits": draw_max_logits(jax.random.fold_in(key_of[5], 71), 0),
        "threshold": jax.random.randint(key_of[4], (1,), 1200, 2001).astype(jnp.int32),
    }


momentum_rate = 0.95
epsilon = 1e-07
coef_one = 3.4445
coef_two = -4.775
coef_three = 2.0315
learn_rate = 0.02
decay_rate = 0.1

def product(left, right):
    return jnp.dot(left, right, precision=lax.Precision.HIGHEST, preferred_element_type=jnp.float32)

def one_layer(grads_layer, momentum, weight, peak, threshold):
    mean_grad = lax.optimization_barrier(jnp.sum(grads_layer.astype(jnp.float32), axis=0)) / N_DP
    new_momentum = momentum_rate * momentum + mean_grad
    blended = mean_grad + momentum_rate * new_momentum
    square_sum = jnp.sum(blended * blended)
    rms_value = jnp.sqrt(square_sum / (F * R))
    ortho = blended / (jnp.sqrt(square_sum) + epsilon)
    for iteration in range(ITERS):
        gram_now = product(ortho.T, ortho)
        poly_mat = coef_two * gram_now + coef_three * product(gram_now, gram_now)
        ortho = coef_one * ortho + product(ortho, poly_mat)
    update = ortho * (0.2 * jnp.sqrt(jnp.float32(max(F, R))))
    stepped = weight * (1.0 - learn_rate * decay_rate) - learn_rate * update
    gamma = jnp.minimum(1.0, threshold[0].astype(jnp.float32) / peak.astype(jnp.float32))
    row_ids = jnp.arange(F, dtype=jnp.int32)
    head_ids = row_ids // (NOPE + VDIM)
    key_rows = row_ids % (NOPE + VDIM) < NOPE
    factor = jnp.where(key_rows, jnp.sqrt(gamma)[head_ids], jnp.float32(1.0))
    return (stepped * factor[:, None], new_momentum, rms_value)

def reference(grads, momentum, weight, max_logits, threshold):
    peak_all = lax.optimization_barrier(jnp.max(max_logits, axis=0))
    masters = []
    moments = []
    rms_list = []
    for layer in range(LAYERS):
        low = layer * F
        master, moment, rms_value = one_layer(grads[:, low:low + F], momentum[low:low + F], weight[low:low + F], peak_all[layer], threshold)
        masters.append(master)
        moments.append(moment)
        rms_list.append(rms_value)
    new_master = jnp.concatenate(masters, axis=0)
    new_momentum = jnp.concatenate(moments, axis=0)
    blend_rms = jnp.repeat(jnp.stack(rms_list), N_COL // LAYERS)
    return (new_master, new_momentum, new_master.astype(jnp.bfloat16), blend_rms)
```

```python
import jax
import jax.numpy as jnp
from jax import lax
from jax.sharding import PartitionSpec as P

R = 512
HEADS = 64
NOPE = 128
VDIM = 128
ITERS = 5
LAYERS = 2
F = 16384


momentum_rate = 0.95
epsilon = 1e-07
coef_one = 3.4445
coef_two = -4.775
coef_three = 2.0315
learn_rate = 0.02
decay_rate = 0.1


def from_partner(value, axis, distance):
    mask = 2**distance
    pairs = [(source, source ^ mask) for source in range(lax.axis_size(axis))]
    return lax.ppermute(value, axis, pairs)


def product(left, right):
    return jnp.dot(left, right, precision=lax.Precision.HIGHEST, preferred_element_type=jnp.float32)


def group_gram(rows_block, span_bits):
    total = lax.psum(product(rows_block.T, rows_block), "dp")
    for bit in range(span_bits):
        total = total + from_partner(total, "col", bit)
    return total


def group_norm(blended, span_bits):
    total = lax.psum(jnp.sum(blended * blended).reshape(1), "dp")
    for bit in range(span_bits):
        total = total + from_partner(total, "col", bit)
    return total[0]


def local(grads, momentum, weight, max_logits, threshold):
    replicas = lax.axis_size("dp")
    span = lax.axis_size("col") // LAYERS
    span_bits = span.bit_length() - 1
    mean_grad = (
        lax.psum_scatter(grads[0].astype(jnp.float32), "dp", scatter_dimension=0, tiled=True)
        / replicas
    )
    new_momentum = momentum_rate * momentum + mean_grad
    blended = mean_grad + momentum_rate * new_momentum
    peak_all = lax.pmax(max_logits[0], "dp")
    col_index = lax.axis_index("col")
    layer = col_index // span
    layer_table = jnp.arange(LAYERS, dtype=jnp.int32)
    peak = jnp.sum(jnp.where(layer_table[:, None] == layer, peak_all, 0), axis=0)
    raw_gram = group_gram(blended, span_bits)
    square_total = jnp.sum(jnp.where(jnp.eye(R, dtype=bool), raw_gram, 0.0))
    blend_rms = jnp.sqrt(square_total / (F * R)).reshape(1)
    inverse = 1.0 / (jnp.sqrt(square_total) + epsilon)
    ortho = blended * inverse
    gram_now = raw_gram * inverse * inverse
    eye = jnp.eye(R, dtype=jnp.float32)
    for iteration in range(ITERS):
        factor = coef_one * eye + coef_two * gram_now + coef_three * product(gram_now, gram_now)
        if iteration < ITERS - 1:
            gram_now = product(product(gram_now, factor), factor)
        ortho = product(ortho, factor)
    update = ortho * (0.2 * jnp.sqrt(jnp.float32(max(F, R))))
    stepped = weight * (1.0 - learn_rate * decay_rate) - learn_rate * update
    row_count = ortho.shape[0]
    first_row = (col_index * replicas + lax.axis_index("dp")) * row_count
    row_ids = (first_row + jnp.arange(row_count, dtype=jnp.int32)) % F
    head_ids = row_ids // (NOPE + VDIM)
    key_rows = row_ids % (NOPE + VDIM) < NOPE
    gamma = jnp.minimum(1.0, threshold[0].astype(jnp.float32) / peak.astype(jnp.float32))
    root_gamma = jnp.sqrt(gamma)
    head_table = jnp.arange(HEADS, dtype=jnp.int32)
    per_row = jnp.sum(
        jnp.where(head_ids[:, None] == head_table[None, :], root_gamma[None, :], jnp.float32(0.0)),
        axis=1,
    )
    factor = jnp.where(key_rows, per_row, jnp.float32(1.0))
    new_master = stepped * factor[:, None]
    new_weight = lax.all_gather(new_master.astype(jnp.bfloat16), "dp", axis=0, tiled=True)
    return (new_master, new_momentum, new_weight, blend_rms)


def solution(mesh):
    return jax.shard_map(
        local,
        mesh=mesh,
        in_specs=(
            P("dp", "col", None),
            P(("col", "dp"), None),
            P(("col", "dp"), None),
            P("dp", None, None),
            P(),
        ),
        out_specs=(P(("col", "dp"), None), P(("col", "dp"), None), P("col", None), P("col")),
        check_vma=False,
    )
```

```python
import functools

import jax
import jax.numpy as jnp
from jax import lax
from jax.experimental import pallas as pl
from jax.experimental.pallas import tpu as pltpu
from jax.sharding import PartitionSpec as P

R = 512
HEADS = 64
NOPE = 128
VDIM = 128
ITERS = 5
LAYERS = 2
F = 16384

NZ = 8
NX = 4
NY = 4
BLOCK = 128
CUT = 80

momentum_rate = 0.95
epsilon = 1e-07
coef_one = 3.4445
coef_two = -4.775
coef_three = 2.0315
learn_rate = 0.02
decay_rate = 0.1

ORDER = (4, -3, 3, -2, 2, -1, 1, 0)
PAIRS = [(i, j) for i in range(4) for j in range(i, 4)]
HALF = len(PAIRS) * BLOCK // 2
PART = HALF // 8
SLAB = PART // 8


def exact(left, right, dims=((1,), (0,))):
    return lax.dot_general(
        left,
        right,
        (dims, ((), ())),
        precision=lax.Precision.HIGHEST,
        preferred_element_type=jnp.float32,
    )


def kernel(
    grads,
    momentum,
    weight,
    max_logits,
    threshold,
    new_master,
    new_momentum,
    new_weight,
    blend_rms,
    own,
    rx,
    relay,
    zs,
    zr,
    packed,
    core_in,
    half_sum,
    xy_in,
    slab_out,
    slab_in,
    slab_sum,
    slab_all,
    full,
    gram,
    factor_mat,
    ortho,
    rounded,
    ml_out,
    ml_x,
    ml_mid,
    ml_z,
    s_local,
    s_x,
    r_x,
    s_z,
    r_z,
    s_ml,
    r_ml,
    s_g,
    r_g,
    s_az,
    r_az,
    s_ax,
    r_ax,
    s_bx,
    r_bx,
    s_bz,
    r_bz,
):
    d = lax.axis_index("dp")
    c = lax.axis_index("col")
    z, x = d // NX, d % NX
    y, core = c // 2, c % 2
    ybase = (y // 2) * 2
    xr, xl, xo = (x + 1) % NX, (x + 3) % NX, (x + 2) % NX
    zup, zdn = (z + 1) % NZ, (z + NZ - 1) % NZ
    m8 = x * 2 + y % 2

    def at_x(xx):
        return (z * NX + xx, c)

    def at_z(zz):
        return (zz * NX + x, c)

    def at_xy(p):
        return (z * NX + p // 2, (ybase + p % 2) * 2 + core)

    partner = (d, y * 2 + 1 - core)

    def send(src, dst, ss, rs, to):
        copy = pltpu.make_async_remote_copy(
            src_ref=src,
            dst_ref=dst,
            send_sem=ss,
            recv_sem=rs,
            device_id=to,
            device_id_type=pl.DeviceIdType.MESH,
        )
        copy.start()
        return copy

    sent = []

    ml_out[...] = jnp.zeros_like(ml_out)
    ml_out[0:2, 0:HEADS] = max_logits[0]

    barrier = pltpu.get_barrier_semaphore()
    mates = [at_xy((m8 + r) % 8) for r in range(1, 8)]
    mates += [at_z((z + r) % NZ) for r in range(1, NZ)]
    mates += [partner]
    for mate in mates:
        pl.semaphore_signal(
            barrier, inc=1, device_id=mate, device_id_type=pl.DeviceIdType.MESH
        )
    own_copy = pltpu.make_async_copy(grads.at[:, x], own, s_local.at[0])
    own_copy.start()
    pl.semaphore_wait(barrier, len(mates))

    chunks = {}
    forwards = {}

    def start_chunk(j):
        zt = (z + ORDER[j] + NZ) % NZ
        chunks[j] = [
            send(grads.at[zt, xo, 0:64], relay.at[j, 0], s_x.at[j, 2], r_x.at[j, 2], at_x(xr)),
            send(grads.at[zt, xo, 64:128], relay.at[j, 1], s_x.at[j, 3], r_x.at[j, 3], at_x(xl)),
            send(grads.at[zt, xr], rx.at[j, 0], s_x.at[j, 0], r_x.at[j, 0], at_x(xr)),
            send(grads.at[zt, xl], rx.at[j, 1], s_x.at[j, 1], r_x.at[j, 1], at_x(xl)),
        ]
        sent.extend(chunks[j])

    def forward_chunk(j):
        chunks[j][0].wait_recv()
        one = send(relay.at[j, 0], rx.at[j, 2, 0:64], s_x.at[j, 4], r_x.at[j, 4], at_x(xr))
        chunks[j][1].wait_recv()
        two = send(relay.at[j, 1], rx.at[j, 2, 64:128], s_x.at[j, 5], r_x.at[j, 5], at_x(xl))
        forwards[j] = [one, two]
        sent.extend(forwards[j])

    ring = {}

    def finish_chunk(j):
        offset = ORDER[j]
        zt = (z + offset + NZ) % NZ
        chunks[j][2].wait_recv()
        chunks[j][3].wait_recv()
        forwards[j][0].wait_recv()
        forwards[j][1].wait_recv()
        value = own[zt].astype(jnp.float32) + rx[j, 0].astype(jnp.float32)
        value = value + (rx[j, 1].astype(jnp.float32) + rx[j, 2].astype(jnp.float32))
        if offset == 4:
            zs[0, 0, 0:64] = value[0:64]
            zs[1, 0, 0:64] = value[64:128]
            for way, to in ((0, zdn), (1, zup)):
                ring[way, 0] = send(
                    zs.at[way, 0, 0:64], zr.at[way, 0, 0:64], s_z.at[way, 0], r_z.at[way, 0], at_z(to)
                )
                sent.append(ring[way, 0])
        elif offset != 0:
            way = 0 if offset < 0 else 1
            to = zdn if offset < 0 else zup
            step = 4 - abs(offset)
            ring[way, step - 1].wait_recv()
            if step == 1:
                part = zr[way, 0, 0:64]
                low = value[0:64] + part if way == 0 else value[0:64]
                high = value[64:128] if way == 0 else value[64:128] + part
                zs[way, 1, 0:64] = low
                zs[way, 1, 64:128] = high
            else:
                zs[way, step] = value + zr[way, step - 1]
            ring[way, step] = send(
                zs.at[way, step], zr.at[way, step], s_z.at[way, step], r_z.at[way, step], at_z(to)
            )
            sent.append(ring[way, step])
        else:
            ring[0, 3].wait_recv()
            ring[1, 3].wait_recv()
            return value + (zr[0, 3] + zr[1, 3])

    start_chunk(0)
    start_chunk(1)
    ml_sends = []
    for r in range(1, NX):
        ml_sends.append(
            send(ml_out, ml_x.at[r - 1], s_ml.at[r - 1], r_ml.at[r - 1], at_x((x + r) % NX))
        )
    sent.extend(ml_sends)
    total = None
    for j in range(8):
        forward_chunk(j)
        if j + 2 < 8:
            start_chunk(j + 2)
        if j == 0:
            own_copy.wait()
        else:
            finish_chunk(j - 1)
        if j == 2:
            for copy in ml_sends:
                copy.wait_recv()
            ml_mid[...] = jnp.maximum(
                jnp.maximum(ml_out[...], ml_x[0]), jnp.maximum(ml_x[1], ml_x[2])
            )
            ml_sends = []
            for r in range(1, NZ):
                ml_sends.append(
                    send(ml_mid, ml_z.at[r - 1], s_ml.at[r + 2], r_ml.at[r + 2], at_z((z + r) % NZ))
                )
            sent.extend(ml_sends)
    total = finish_chunk(7)

    mean_grad = total * (1.0 / (NZ * NX))
    moment = momentum_rate * momentum[...] + mean_grad
    new_momentum[...] = moment
    blended = mean_grad + momentum_rate * moment
    ortho[...] = blended

    low = 0
    for i in range(4):
        strip = exact(ortho[:, i * BLOCK : (i + 1) * BLOCK], ortho[:, i * BLOCK :], ((0,), (0,)))
        for j in range(i, 4):
            packed[low * BLOCK : (low + 1) * BLOCK] = strip[:, (j - i) * BLOCK : (j - i + 1) * BLOCK]
            low += 1
    theirs = pl.ds(pl.multiple_of((1 - core) * HALF, BLOCK // 2), HALF)
    mine = pl.ds(pl.multiple_of(core * HALF, BLOCK // 2), HALF)
    copy = send(packed.at[theirs], core_in, s_g.at[0], r_g.at[0], partner)
    sent.append(copy)
    copy.wait_recv()
    half_sum[...] = packed[mine] + core_in[...]

    copies = []
    for r in range(1, 8):
        p = (m8 + r) % 8
        piece = pl.ds(pl.multiple_of(p * PART, 8), PART)
        copies.append(send(half_sum.at[piece], xy_in.at[r - 1], s_g.at[r], r_g.at[r], at_xy(p)))
    sent.extend(copies)
    my_piece = pl.ds(pl.multiple_of(m8 * PART, 8), PART)
    part = half_sum[my_piece]
    for r in range(1, 8):
        copies[r - 1].wait_recv()
        part = part + xy_in[r - 1]
    for i in range(8):
        slab_out[i] = part[i * SLAB : (i + 1) * SLAB]
    copies = []
    for r in range(1, NZ):
        zt = (z + r) % NZ
        copies.append(
            send(slab_out.at[zt], slab_in.at[r - 1], s_g.at[7 + r], r_g.at[7 + r], at_z(zt))
        )
    sent.extend(copies)
    slab = slab_out[z]
    for r in range(1, NZ):
        copies[r - 1].wait_recv()
        slab = slab + slab_in[r - 1]
    slab_sum[...] = slab
    slab_all[z] = slab
    copies = []
    for r in range(1, NZ):
        zt = (z + r) % NZ
        copies.append(
            send(slab_sum, slab_all.at[z], s_g.at[14 + r], r_g.at[14 + r], at_z(zt))
        )
    sent.extend(copies)
    for copy in copies:
        copy.wait_recv()
    here = pl.ds(pl.multiple_of(core * HALF + m8 * PART, 8), PART)
    full[here] = jnp.concatenate([slab_all[i] for i in range(8)], axis=0)
    copies = []
    for r in range(1, 8):
        p = (m8 + r) % 8
        copies.append(send(full.at[here], full.at[here], s_g.at[21 + r], r_g.at[21 + r], at_xy(p)))
    sent.extend(copies)
    for copy in copies:
        copy.wait_recv()
    copy = send(full.at[mine], full.at[mine], s_g.at[29], r_g.at[29], partner)
    sent.append(copy)
    copy.wait_recv()

    rows = lax.broadcasted_iota(jnp.int32, (BLOCK, BLOCK), 0)
    cols = lax.broadcasted_iota(jnp.int32, (BLOCK, BLOCK), 1)
    diagonal = jnp.zeros((BLOCK, BLOCK), jnp.float32)
    for low, (i, j) in enumerate(PAIRS):
        if i == j:
            block = full[low * BLOCK : (low + 1) * BLOCK]
            diagonal = diagonal + jnp.where(rows == cols, block, 0.0)
    square_total = jnp.sum(jnp.sum(diagonal, axis=0, keepdims=True), axis=1, keepdims=True)
    inverse = 1.0 / (jnp.sqrt(square_total) + epsilon)
    blend_rms[0] = jnp.sqrt(square_total * (1.0 / (F * R)))[0, 0]
    for low, (i, j) in enumerate(PAIRS):
        block = full[low * BLOCK : (low + 1) * BLOCK] * inverse * inverse
        gram[i * BLOCK : (i + 1) * BLOCK, j * BLOCK : (j + 1) * BLOCK] = block
        if i != j:
            gram[j * BLOCK : (j + 1) * BLOCK, i * BLOCK : (i + 1) * BLOCK] = block.T
    ortho[...] = ortho[...] * inverse

    def fill_factor():
        now = gram[...]
        square = exact(now, now)
        row_ids = lax.broadcasted_iota(jnp.int32, (R, R), 0)
        col_ids = lax.broadcasted_iota(jnp.int32, (R, R), 1)
        factor_mat[...] = (
            jnp.where(row_ids == col_ids, coef_one, 0.0) + coef_two * now + coef_three * square
        )

    def step(k, carry):
        fill_factor()
        gram[...] = exact(gram[...], factor_mat[...])
        gram[...] = exact(gram[...], factor_mat[...])
        ortho[...] = exact(ortho[...], factor_mat[...])
        return carry

    lax.fori_loop(0, ITERS - 1, step, 0)
    fill_factor()
    last = exact(ortho[...], factor_mat[...])

    for copy in ml_sends:
        copy.wait_recv()
    peaks = ml_mid[...]
    for r in range(NZ - 1):
        peaks = jnp.maximum(peaks, ml_z[r])
    head = (c % (2 * NY // LAYERS)) * (HEADS * LAYERS // (2 * NY)) + d // 2
    layer = c // (2 * NY // LAYERS)
    rows = lax.broadcasted_iota(jnp.int32, (8, 128), 0)
    cols = lax.broadcasted_iota(jnp.int32, (8, 128), 1)
    chosen = jnp.where((rows == layer) & (cols == head), peaks, 0)
    peak = jnp.max(jnp.max(chosen, axis=0, keepdims=True), axis=1, keepdims=True)
    limit = jnp.full((1, 1), threshold[0], jnp.int32).astype(jnp.float32)
    gamma = jnp.minimum(1.0, limit / peak.astype(jnp.float32))
    scale = jnp.where(jnp.full((1, 1), d % 2, jnp.int32) == 0, jnp.sqrt(gamma), 1.0)
    update = last * (0.2 * float(max(F, R)) ** 0.5)
    stepped = weight[...] * (1.0 - learn_rate * decay_rate) - learn_rate * update
    master = stepped * scale
    new_master[...] = master
    rounded[...] = master.astype(jnp.bfloat16)

    local_copy = pltpu.make_async_copy(rounded, new_weight.at[z, x], s_local.at[1])
    local_copy.start()
    bx = [
        send(rounded.at[CUT:BLOCK], new_weight.at[z, x, CUT:BLOCK], s_bx.at[0], r_bx.at[0], at_x(xr)),
        send(rounded.at[CUT:BLOCK], new_weight.at[z, x, CUT:BLOCK], s_bx.at[1], r_bx.at[1], at_x(xl)),
    ]
    az = {}
    az[0, 0] = send(rounded.at[0:CUT], new_weight.at[z, x, 0:CUT], s_az.at[0, 0], r_az.at[0, 0], at_z(zup))
    az[1, 0] = send(rounded.at[0:CUT], new_weight.at[z, x, 0:CUT], s_az.at[1, 0], r_az.at[1, 0], at_z(zdn))

    ax = {}

    def spread(slot, zz, src):
        ax[slot] = [
            send(src, new_weight.at[zz, x, 0:CUT], s_ax.at[slot, 0], r_ax.at[slot, 0], at_x(xr)),
            send(src, new_weight.at[zz, x, 0:CUT], s_ax.at[slot, 1], r_ax.at[slot, 1], at_x(xl)),
        ]
        sent.extend(ax[slot])

    def spread_on(slot, zz):
        ax[slot][0].wait_recv()
        left = new_weight.at[zz, xl, 0:48]
        one = send(left, left, s_ax.at[slot, 2], r_ax.at[slot, 2], at_x(xr))
        ax[slot][1].wait_recv()
        right = new_weight.at[zz, xr, 48:CUT]
        two = send(right, right, s_ax.at[slot, 3], r_ax.at[slot, 3], at_x(xl))
        ax[slot].extend([one, two])
        sent.extend([one, two])

    spread(0, z, rounded.at[0:CUT])
    bx[0].wait_recv()
    left = new_weight.at[z, xl, CUT : CUT + 32]
    bx.append(send(left, left, s_bx.at[2], r_bx.at[2], at_x(xr)))
    bx[1].wait_recv()
    right = new_weight.at[z, xr, CUT + 32 : BLOCK]
    bx.append(send(right, right, s_bx.at[3], r_bx.at[3], at_x(xl)))
    local_copy.wait()
    bx[2].wait_recv()
    bx[3].wait_recv()
    sent.extend(bx)
    bz = {}

    def ring_b(step):
        if step < 3:
            up = new_weight.at[(z + NZ - step) % NZ, :, CUT:BLOCK]
            down = new_weight.at[(z + step) % NZ, :, CUT:BLOCK]
        else:
            up = new_weight.at[(z + NZ - step) % NZ, 0:2, CUT:BLOCK]
            down = new_weight.at[(z + step) % NZ, 2:4, CUT:BLOCK]
        bz[0, step] = send(up, up, s_bz.at[0, step], r_bz.at[0, step], at_z(zup))
        bz[1, step] = send(down, down, s_bz.at[1, step], r_bz.at[1, step], at_z(zdn))
        sent.extend([bz[0, step], bz[1, step]])

    def ring_a(step):
        if step < 3:
            up = new_weight.at[(z + NZ - step) % NZ, x, 0:CUT]
            down = new_weight.at[(z + step) % NZ, x, 0:CUT]
        else:
            up = new_weight.at[(z + NZ - step) % NZ, x, 0:48]
            down = new_weight.at[(z + step) % NZ, x, 48:CUT]
        az[0, step] = send(up, up, s_az.at[0, step], r_az.at[0, step], at_z(zup))
        az[1, step] = send(down, down, s_az.at[1, step], r_az.at[1, step], at_z(zdn))

    ring_b(0)
    for step in range(1, 4):
        az[0, step - 1].wait_recv()
        az[1, step - 1].wait_recv()
        ring_a(step)
        up, down = (z + NZ - step) % NZ, (z + step) % NZ
        spread(2 * step - 1, up, new_weight.at[up, x, 0:CUT])
        spread(2 * step, down, new_weight.at[down, x, 0:CUT])
        if step == 1:
            spread_on(0, z)
        else:
            spread_on(2 * step - 3, (z + NZ - step + 1) % NZ)
            spread_on(2 * step - 2, (z + step - 1) % NZ)
        bz[0, step - 1].wait_recv()
        bz[1, step - 1].wait_recv()
        ring_b(step)
    az[0, 3].wait_recv()
    az[1, 3].wait_recv()
    far = (z + 4) % NZ
    spread(7, far, new_weight.at[far, x, 0:CUT])
    spread_on(5, (z + NZ - 3) % NZ)
    spread_on(6, (z + 3) % NZ)
    spread_on(7, far)
    bz[0, 3].wait_recv()
    bz[1, 3].wait_recv()
    for slot in range(8):
        ax[slot][2].wait_recv()
        ax[slot][3].wait_recv()
    sent.extend(az.values())
    for copy in sent:
        copy.wait_send()


def local(grads, momentum, weight, max_logits, threshold):
    vmem = pl.BlockSpec(memory_space=pltpu.VMEM)
    smem = pl.BlockSpec(memory_space=pltpu.SMEM)
    hbm = pl.BlockSpec(memory_space=pl.ANY)
    f32, bf16, i32 = jnp.float32, jnp.bfloat16, jnp.int32
    dma = pltpu.SemaphoreType.DMA
    new_master, new_momentum, new_weight, blend_rms = pl.pallas_call(
        kernel,
        out_shape=(
            jax.ShapeDtypeStruct((BLOCK, R), f32),
            jax.ShapeDtypeStruct((BLOCK, R), f32),
            jax.ShapeDtypeStruct((NZ, NX, BLOCK, R), bf16),
            jax.ShapeDtypeStruct((1,), f32),
        ),
        in_specs=[hbm, vmem, vmem, vmem, smem],
        out_specs=(vmem, vmem, hbm, smem),
        scratch_shapes=[
            pltpu.VMEM((NZ, BLOCK, R), bf16),
            pltpu.VMEM((8, 3, BLOCK, R), bf16),
            pltpu.VMEM((8, 2, BLOCK // 2, R), bf16),
            pltpu.VMEM((2, 4, BLOCK, R), f32),
            pltpu.VMEM((2, 4, BLOCK, R), f32),
            pltpu.VMEM((2 * HALF, BLOCK), f32),
            pltpu.VMEM((HALF, BLOCK), f32),
            pltpu.VMEM((HALF, BLOCK), f32),
            pltpu.VMEM((7, PART, BLOCK), f32),
            pltpu.VMEM((8, SLAB, BLOCK), f32),
            pltpu.VMEM((7, SLAB, BLOCK), f32),
            pltpu.VMEM((SLAB, BLOCK), f32),
            pltpu.VMEM((8, SLAB, BLOCK), f32),
            pltpu.VMEM((2 * HALF, BLOCK), f32),
            pltpu.VMEM((R, R), f32),
            pltpu.VMEM((R, R), f32),
            pltpu.VMEM((BLOCK, R), f32),
            pltpu.VMEM((BLOCK, R), bf16),
            pltpu.VMEM((8, 128), i32),
            pltpu.VMEM((3, 8, 128), i32),
            pltpu.VMEM((8, 128), i32),
            pltpu.VMEM((7, 8, 128), i32),
            dma((2,)),
            dma((8, 6)),
            dma((8, 6)),
            dma((2, 4)),
            dma((2, 4)),
            dma((10,)),
            dma((10,)),
            dma((30,)),
            dma((30,)),
            dma((2, 4)),
            dma((2, 4)),
            dma((8, 4)),
            dma((8, 4)),
            dma((4,)),
            dma((4,)),
            dma((2, 4)),
            dma((2, 4)),
        ],
        compiler_params=pltpu.CompilerParams(
            collective_id=0, has_side_effects=True, vmem_limit_bytes=48 * 1024 * 1024
        ),
        name="muon",
    )(grads.reshape(NZ, NX, BLOCK, R), momentum, weight, max_logits, threshold)
    return (new_master, new_momentum, new_weight.reshape(NZ * NX * BLOCK, R), blend_rms)


def solution(mesh):
    return jax.shard_map(
        local,
        mesh=mesh,
        in_specs=(
            P("dp", "col", None),
            P(("col", "dp"), None),
            P(("col", "dp"), None),
            P("dp", None, None),
            P(),
        ),
        out_specs=(P(("col", "dp"), None), P(("col", "dp"), None), P("col", None), P("col")),
        check_vma=False,
    )
```

```python
import functools

import jax
import jax.numpy as jnp
from jax import lax
from jax.experimental import pallas as pl
from jax.experimental.pallas import tpu as pltpu
from jax.sharding import PartitionSpec as P

R = 512
HEADS = 64
NOPE = 128
VDIM = 128
ITERS = 5
LAYERS = 2
F = 16384

NZ = 8
NX = 4
NY = 4
BLOCK = 128
CUT = 80
CA = 384
CB = R - CA
FINE = 2

momentum_rate = 0.95
epsilon = 1e-07
coef_one = 3.4445
coef_two = -4.775
coef_three = 2.0315
learn_rate = 0.02
decay_rate = 0.1

ORDER = (4, -3, 3, -2, 2, -1, 1, 0)
PAIRS = [(i, j) for i in range(4) for j in range(i, 4)]
HALF = len(PAIRS) * BLOCK // 2
PART = HALF // 8
SLAB = PART // 8


def exact(left, right, dims=((1,), (0,))):
    return lax.dot_general(
        left,
        right,
        (dims, ((), ())),
        precision=lax.Precision.HIGHEST,
        preferred_element_type=jnp.float32,
    )


def halves(value, count):
    terms = []
    for left in range(count, 0, -1):
        terms.append(value.astype(jnp.bfloat16))
        if left > 1:
            value = value - terms[-1].astype(jnp.float32)
    return terms


def split_product(left, right):
    def dot(i, j):
        return jnp.dot(left[i], right[j], preferred_element_type=jnp.float32)

    total = dot(0, 1) + dot(1, 0)
    if len(left) == 3:
        total = total + (dot(1, 1) + (dot(0, 2) + dot(2, 0)))
    return dot(0, 0) + total


def mirrored(left, right):
    half = R // 2
    top = split_product([term[0:half] for term in left], right)
    low = split_product([term[half:R] for term in left], [term[:, half:R] for term in right])
    return jnp.concatenate([top, jnp.concatenate([top[:, half:R].T, low], axis=1)], axis=0)


def kernel(
    grads,
    momentum,
    weight,
    max_logits,
    threshold,
    new_master,
    new_momentum,
    new_weight,
    blend_rms,
    own,
    own_b,
    rx,
    zs,
    zr,
    bs,
    br,
    b_sum,
    b_in,
    moment_in,
    weight_in,
    moment_out,
    master_out,
    ml_in,
    packed,
    core_in,
    half_sum,
    xy_in,
    slab_out,
    slab_in,
    slab_sum,
    slab_all,
    full,
    gram,
    ortho,
    rounded,
    ml_out,
    ml_x,
    ml_mid,
    ml_z,
    s_local,
    s_x,
    r_x,
    s_z,
    r_z,
    s_b,
    r_b,
    s_ml,
    r_ml,
    s_g,
    r_g,
    s_az,
    r_az,
    s_ax,
    r_ax,
    s_bx,
    r_bx,
    s_bz,
    r_bz,
):
    d = lax.axis_index("dp")
    c = lax.axis_index("col")
    z, x = d // NX, d % NX
    y, core = c // 2, c % 2
    ybase = (y // 2) * 2
    xr, xl, xo = (x + 1) % NX, (x + 3) % NX, (x + 2) % NX
    zup, zdn = (z + 1) % NZ, (z + NZ - 1) % NZ
    m8 = x * 2 + y % 2

    def at_x(xx):
        return (z * NX + xx, c)

    def at_z(zz):
        return (zz * NX + x, c)

    def at_xy(p):
        return (z * NX + p // 2, (ybase + p % 2) * 2 + core)

    partner = (d, y * 2 + 1 - core)

    def send(src, dst, ss, rs, to):
        copy = pltpu.make_async_remote_copy(
            src_ref=src,
            dst_ref=dst,
            send_sem=ss,
            recv_sem=rs,
            device_id=to,
            device_id_type=pl.DeviceIdType.MESH,
        )
        copy.start()
        return copy

    sent = []

    barrier = pltpu.get_barrier_semaphore()
    mates = [at_xy((m8 + r) % 8) for r in range(1, 8)]
    mates += [at_z((z + r) % NZ) for r in range(1, NZ)]
    mates += [partner]
    for mate in mates:
        pl.semaphore_signal(
            barrier, inc=1, device_id=mate, device_id_type=pl.DeviceIdType.MESH
        )
    loads = [
        pltpu.make_async_copy(grads.at[:, :, :, CA:R], own_b, s_local.at[0]),
        pltpu.make_async_copy(grads.at[:, x, :, 0:CA], own, s_local.at[1]),
        pltpu.make_async_copy(max_logits, ml_in, s_local.at[2]),
        pltpu.make_async_copy(momentum, moment_in, s_local.at[3]),
        pltpu.make_async_copy(weight, weight_in, s_local.at[4]),
    ]
    for copy in loads:
        copy.start()
    pl.semaphore_wait(barrier, len(mates))

    chunks = {}

    def start_chunk(j):
        zt = (z + ORDER[j] + NZ) % NZ
        chunks[j] = []
        for r in (1, 3, 2):
            xt = (x + r) % NX
            chunks[j].append(
                send(
                    grads.at[zt, xt, :, 0:CA],
                    rx.at[j, r - 1],
                    s_x.at[j, r - 1],
                    r_x.at[j, r - 1],
                    at_x(xt),
                )
            )
        sent.extend(chunks[j])

    ring = {}

    def finish_chunk(j):
        offset = ORDER[j]
        zt = (z + offset + NZ) % NZ
        for copy in chunks[j]:
            copy.wait_recv()
        value = own[zt].astype(jnp.float32) + rx[j, 0].astype(jnp.float32)
        value = value + (rx[j, 1].astype(jnp.float32) + rx[j, 2].astype(jnp.float32))
        if offset == 4:
            zs[0, 0, 0:64] = value[0:64]
            zs[1, 0, 0:64] = value[64:128]
            for way, to in ((0, zdn), (1, zup)):
                ring[way, 0] = send(
                    zs.at[way, 0, 0:64], zr.at[way, 0, 0:64], s_z.at[way, 0], r_z.at[way, 0], at_z(to)
                )
                sent.append(ring[way, 0])
        elif offset != 0:
            way = 0 if offset < 0 else 1
            to = zdn if offset < 0 else zup
            step = 4 - abs(offset)
            ring[way, step - 1].wait_recv()
            if step == 1:
                part = zr[way, 0, 0:64]
                zs[way, 1, 0:64] = value[0:64] + part if way == 0 else value[0:64]
                zs[way, 1, 64:128] = value[64:128] if way == 0 else value[64:128] + part
            else:
                zs[way, step] = value + zr[way, step - 1]
            ring[way, step] = send(
                zs.at[way, step], zr.at[way, step], s_z.at[way, step], r_z.at[way, step], at_z(to)
            )
            sent.append(ring[way, step])
        else:
            ring[0, 3].wait_recv()
            ring[1, 3].wait_recv()
            return value + (zr[0, 3] + zr[1, 3])

    wheel = {}

    def turn(step):
        for way, to in ((0, zdn), (1, zup)):
            sign = -1 if way == 0 else 1
            zt = (z + sign * (4 - step) + NZ) % NZ
            lo, up = 2 * way, 2 * way + 2
            if step == 0:
                bs[way, 0, lo:up] = own_b[zt, lo:up].astype(jnp.float32)
                src, dst = bs.at[way, 0, lo:up], br.at[way, 0, lo:up]
            else:
                wheel[way, step - 1].wait_recv()
                if step == 1:
                    rest = 2 - lo
                    bs[way, 1, lo:up] = own_b[zt, lo:up].astype(jnp.float32) + br[way, 0, lo:up]
                    bs[way, 1, rest : rest + 2] = own_b[zt, rest : rest + 2].astype(jnp.float32)
                else:
                    bs[way, step] = own_b[zt].astype(jnp.float32) + br[way, step - 1]
                src, dst = bs.at[way, step], br.at[way, step]
            wheel[way, step] = send(src, dst, s_b.at[way, step], r_b.at[way, step], at_z(to))
            sent.append(wheel[way, step])

    start_chunk(0)
    start_chunk(1)
    loads[0].wait()
    turn(0)
    start_chunk(2)
    loads[2].wait()
    ml_out[...] = jnp.zeros_like(ml_out)
    ml_out[0:2, 0:HEADS] = ml_in[0]
    ml_sends = []
    for r in range(1, NX):
        ml_sends.append(
            send(ml_out, ml_x.at[r - 1], s_ml.at[r - 1], r_ml.at[r - 1], at_x((x + r) % NX))
        )
    sent.extend(ml_sends)
    loads[1].wait()
    cross = []
    for j in range(7):
        finish_chunk(j)
        if j + 3 < 8:
            start_chunk(j + 3)
        if j in (0, 2, 4):
            turn(j // 2 + 1)
        if j == 3:
            for copy in ml_sends:
                copy.wait_recv()
            ml_mid[...] = jnp.maximum(
                jnp.maximum(ml_out[...], ml_x[0]), jnp.maximum(ml_x[1], ml_x[2])
            )
            ml_sends = []
            for r in range(1, NZ):
                ml_sends.append(
                    send(ml_mid, ml_z.at[r - 1], s_ml.at[r + 2], r_ml.at[r + 2], at_z((z + r) % NZ))
                )
            sent.extend(ml_sends)
        if j == 5:
            wheel[0, 3].wait_recv()
            wheel[1, 3].wait_recv()
            b_sum[...] = own_b[z].astype(jnp.float32) + (br[0, 3] + br[1, 3])
            for r in range(1, NX):
                xt = (x + r) % NX
                cross.append(
                    send(b_sum.at[xt], b_in.at[r - 1], s_b.at[2, r - 1], r_b.at[2, r - 1], at_x(xt))
                )
            sent.extend(cross)
    total_a = finish_chunk(7)
    loads[3].wait()
    loads[4].wait()
    total_b = b_sum[x]
    for r in range(1, NX):
        cross[r - 1].wait_recv()
        total_b = total_b + b_in[r - 1]

    for total, span in ((total_a, slice(0, CA)), (total_b, slice(CA, R))):
        mean_grad = total * (1.0 / (NZ * NX))
        moment = momentum_rate * moment_in[:, span] + mean_grad
        moment_out[:, span] = moment
        ortho[:, span] = mean_grad + momentum_rate * moment
    stores = [pltpu.make_async_copy(moment_out, new_momentum, s_local.at[5])]
    stores[0].start()

    low = 0
    for i in range(4):
        strip = exact(ortho[:, i * BLOCK : (i + 1) * BLOCK], ortho[:, i * BLOCK :], ((0,), (0,)))
        for j in range(i, 4):
            packed[low * BLOCK : (low + 1) * BLOCK] = strip[:, (j - i) * BLOCK : (j - i + 1) * BLOCK]
            low += 1
    theirs = pl.ds(pl.multiple_of((1 - core) * HALF, BLOCK // 2), HALF)
    mine = pl.ds(pl.multiple_of(core * HALF, BLOCK // 2), HALF)
    copy = send(packed.at[theirs], core_in, s_g.at[0], r_g.at[0], partner)
    sent.append(copy)
    copy.wait_recv()
    half_sum[...] = packed[mine] + core_in[...]

    copies = []
    for r in range(1, 8):
        p = (m8 + r) % 8
        piece = pl.ds(pl.multiple_of(p * PART, 8), PART)
        copies.append(send(half_sum.at[piece], xy_in.at[r - 1], s_g.at[r], r_g.at[r], at_xy(p)))
    sent.extend(copies)
    my_piece = pl.ds(pl.multiple_of(m8 * PART, 8), PART)
    part = half_sum[my_piece]
    for r in range(1, 8):
        copies[r - 1].wait_recv()
        part = part + xy_in[r - 1]
    for i in range(8):
        slab_out[i] = part[i * SLAB : (i + 1) * SLAB]
    copies = []
    for r in range(1, NZ):
        zt = (z + r) % NZ
        copies.append(
            send(slab_out.at[zt], slab_in.at[r - 1], s_g.at[7 + r], r_g.at[7 + r], at_z(zt))
        )
    sent.extend(copies)
    slab = slab_out[z]
    for r in range(1, NZ):
        copies[r - 1].wait_recv()
        slab = slab + slab_in[r - 1]
    slab_sum[...] = slab
    slab_all[z] = slab
    copies = []
    for r in range(1, NZ):
        zt = (z + r) % NZ
        copies.append(
            send(slab_sum, slab_all.at[z], s_g.at[14 + r], r_g.at[14 + r], at_z(zt))
        )
    sent.extend(copies)
    for copy in copies:
        copy.wait_recv()
    here = pl.ds(pl.multiple_of(core * HALF + m8 * PART, 8), PART)
    full[here] = jnp.concatenate([slab_all[i] for i in range(8)], axis=0)
    copies = []
    for r in range(1, 8):
        p = (m8 + r) % 8
        copies.append(send(full.at[here], full.at[here], s_g.at[21 + r], r_g.at[21 + r], at_xy(p)))
    sent.extend(copies)
    for copy in copies:
        copy.wait_recv()
    copy = send(full.at[mine], full.at[mine], s_g.at[29], r_g.at[29], partner)
    sent.append(copy)
    copy.wait_recv()

    rows = lax.broadcasted_iota(jnp.int32, (BLOCK, BLOCK), 0)
    cols = lax.broadcasted_iota(jnp.int32, (BLOCK, BLOCK), 1)
    diagonal = jnp.zeros((BLOCK, BLOCK), jnp.float32)
    for low, (i, j) in enumerate(PAIRS):
        if i == j:
            block = full[low * BLOCK : (low + 1) * BLOCK]
            diagonal = diagonal + jnp.where(rows == cols, block, 0.0)
    square_total = jnp.sum(jnp.sum(diagonal, axis=0, keepdims=True), axis=1, keepdims=True)
    inverse = 1.0 / (jnp.sqrt(square_total) + epsilon)
    blend_rms[0] = jnp.sqrt(square_total * (1.0 / (F * R)))[0, 0]
    for low, (i, j) in enumerate(PAIRS):
        block = full[low * BLOCK : (low + 1) * BLOCK] * inverse * inverse
        gram[i * BLOCK : (i + 1) * BLOCK, j * BLOCK : (j + 1) * BLOCK] = block
        if i != j:
            gram[j * BLOCK : (j + 1) * BLOCK, i * BLOCK : (i + 1) * BLOCK] = block.T
    ortho[...] = ortho[...] * inverse

    def step(count, k, carry):
        now = halves(gram[...], count)
        square = mirrored(now, now)
        row_ids = lax.broadcasted_iota(jnp.int32, (R, R), 0)
        col_ids = lax.broadcasted_iota(jnp.int32, (R, R), 1)
        factor = halves(
            jnp.where(row_ids == col_ids, coef_one, 0.0) + coef_two * gram[...] + coef_three * square,
            count,
        )
        ortho[...] = split_product(halves(ortho[...], count), factor)
        if k is not None:
            once = halves(mirrored(now, factor), count)
            gram[...] = mirrored(once, factor)
        return carry

    lax.fori_loop(0, FINE, functools.partial(step, 3), 0)
    lax.fori_loop(FINE, ITERS - 1, functools.partial(step, 2), 0)
    step(2, None, 0)
    last = ortho[...]

    for copy in ml_sends:
        copy.wait_recv()
    peaks = ml_mid[...]
    for r in range(NZ - 1):
        peaks = jnp.maximum(peaks, ml_z[r])
    head = (c % (2 * NY // LAYERS)) * (HEADS * LAYERS // (2 * NY)) + d // 2
    layer = c // (2 * NY // LAYERS)
    rows = lax.broadcasted_iota(jnp.int32, (8, 128), 0)
    cols = lax.broadcasted_iota(jnp.int32, (8, 128), 1)
    chosen = jnp.where((rows == layer) & (cols == head), peaks, 0)
    peak = jnp.max(jnp.max(chosen, axis=0, keepdims=True), axis=1, keepdims=True)
    limit = jnp.full((1, 1), threshold[0], jnp.int32).astype(jnp.float32)
    gamma = jnp.minimum(1.0, limit / peak.astype(jnp.float32))
    scale = jnp.where(jnp.full((1, 1), d % 2, jnp.int32) == 0, jnp.sqrt(gamma), 1.0)
    update = last * (0.2 * float(max(F, R)) ** 0.5)
    stepped = weight_in[...] * (1.0 - learn_rate * decay_rate) - learn_rate * update
    master = stepped * scale
    master_out[...] = master
    stores.append(pltpu.make_async_copy(master_out, new_master, s_local.at[6]))
    rounded[...] = master.astype(jnp.bfloat16)

    stores.append(pltpu.make_async_copy(rounded, new_weight.at[z, x], s_local.at[7]))
    bx, az, ax, bz = [], {}, {}, {}
    for r in (1, 3, 2):
        bx.append(
            send(
                rounded.at[CUT:BLOCK],
                new_weight.at[z, x, CUT:BLOCK],
                s_bx.at[r - 1],
                r_bx.at[r - 1],
                at_x((x + r) % NX),
            )
        )

    def ring_a(step):
        up, down = (z + NZ - step) % NZ, (z + step) % NZ
        if step == 0:
            sources = [rounded.at[0:CUT], rounded.at[0:CUT]]
            spans = [(0, CUT), (0, CUT)]
        else:
            spans = [(0, CUT), (0, CUT)] if step < 3 else [(0, 48), (48, CUT)]
            sources = [
                new_weight.at[up, x, spans[0][0] : spans[0][1]],
                new_weight.at[down, x, spans[1][0] : spans[1][1]],
            ]
        for way, zz, to in ((0, up, zup), (1, down, zdn)):
            lo, hi = spans[way]
            az[way, step] = send(
                sources[way], new_weight.at[zz, x, lo:hi], s_az.at[way, step], r_az.at[way, step], at_z(to)
            )

    def ring_b(step):
        up, down = (z + NZ - step) % NZ, (z + step) % NZ
        for half in range(2):
            for way, zz, to in ((0, up, zup), (1, down, zdn)):
                if step > 0:
                    bz[way, step - 1, half].wait_recv()
                if step == 3 and half != way:
                    continue
                piece = new_weight.at[zz, 2 * half : 2 * half + 2, CUT:BLOCK]
                bz[way, step, half] = send(
                    piece, piece, s_bz.at[way, step, half], r_bz.at[way, step, half], at_z(to)
                )

    def spread(slot, zz, src):
        ax[slot] = [
            send(src, new_weight.at[zz, x, 0:CUT], s_ax.at[slot, 0], r_ax.at[slot, 0], at_x(xr)),
            send(src, new_weight.at[zz, x, 0:CUT], s_ax.at[slot, 1], r_ax.at[slot, 1], at_x(xl)),
        ]

    def spread_on(slot, zz):
        ax[slot][0].wait_recv()
        left = new_weight.at[zz, xl, 0:48]
        ax[slot].append(send(left, left, s_ax.at[slot, 2], r_ax.at[slot, 2], at_x(xr)))
        ax[slot][1].wait_recv()
        right = new_weight.at[zz, xr, 48:CUT]
        ax[slot].append(send(right, right, s_ax.at[slot, 3], r_ax.at[slot, 3], at_x(xl)))

    ring_a(0)
    spread(0, z, rounded.at[0:CUT])
    stores[1].start()
    stores[2].start()
    for copy in sent:
        copy.wait_send()
    places = [z]
    for step in range(1, 5):
        az[0, step - 1].wait_recv()
        az[1, step - 1].wait_recv()
        up, down = (z + NZ - step) % NZ, (z + step) % NZ
        if step < 4:
            ring_a(step)
            spread(2 * step - 1, up, new_weight.at[up, x, 0:CUT])
            spread(2 * step, down, new_weight.at[down, x, 0:CUT])
            places.extend([up, down])
        else:
            spread(7, up, new_weight.at[up, x, 0:CUT])
            places.append(up)
        if step == 1:
            stores[2].wait()
            for copy in bx:
                copy.wait_recv()
        elif step == 2:
            spread_on(0, z)
        else:
            spread_on(2 * step - 5, places[2 * step - 5])
            spread_on(2 * step - 4, places[2 * step - 4])
        ring_b(step - 1)
    for slot in range(5, 8):
        spread_on(slot, places[slot])
    bz[0, 3, 0].wait_recv()
    bz[1, 3, 1].wait_recv()
    for slot in range(8):
        ax[slot][2].wait_recv()
        ax[slot][3].wait_recv()
    for copies in (bx, az.values(), bz.values(), *ax.values()):
        for copy in copies:
            copy.wait_send()
    stores[0].wait()
    stores[1].wait()


def local(grads, momentum, weight, max_logits, threshold):
    smem = pl.BlockSpec(memory_space=pltpu.SMEM)
    hbm = pl.BlockSpec(memory_space=pl.ANY)
    f32, bf16, i32 = jnp.float32, jnp.bfloat16, jnp.int32
    dma = pltpu.SemaphoreType.DMA
    new_master, new_momentum, new_weight, blend_rms = pl.pallas_call(
        kernel,
        out_shape=(
            jax.ShapeDtypeStruct((BLOCK, R), f32),
            jax.ShapeDtypeStruct((BLOCK, R), f32),
            jax.ShapeDtypeStruct((NZ, NX, BLOCK, R), bf16),
            jax.ShapeDtypeStruct((1,), f32),
        ),
        in_specs=[hbm, hbm, hbm, hbm, smem],
        out_specs=(hbm, hbm, hbm, smem),
        scratch_shapes=[
            pltpu.VMEM((NZ, BLOCK, CA), bf16),
            pltpu.VMEM((NZ, NX, BLOCK, CB), bf16),
            pltpu.VMEM((8, 3, BLOCK, CA), bf16),
            pltpu.VMEM((2, 4, BLOCK, CA), f32),
            pltpu.VMEM((2, 4, BLOCK, CA), f32),
            pltpu.VMEM((2, 4, NX, BLOCK, CB), f32),
            pltpu.VMEM((2, 4, NX, BLOCK, CB), f32),
            pltpu.VMEM((NX, BLOCK, CB), f32),
            pltpu.VMEM((3, BLOCK, CB), f32),
            pltpu.VMEM((BLOCK, R), f32),
            pltpu.VMEM((BLOCK, R), f32),
            pltpu.VMEM((BLOCK, R), f32),
            pltpu.VMEM((BLOCK, R), f32),
            pltpu.VMEM((1, LAYERS, HEADS), i32),
            pltpu.VMEM((2 * HALF, BLOCK), f32),
            pltpu.VMEM((HALF, BLOCK), f32),
            pltpu.VMEM((HALF, BLOCK), f32),
            pltpu.VMEM((7, PART, BLOCK), f32),
            pltpu.VMEM((8, SLAB, BLOCK), f32),
            pltpu.VMEM((7, SLAB, BLOCK), f32),
            pltpu.VMEM((SLAB, BLOCK), f32),
            pltpu.VMEM((8, SLAB, BLOCK), f32),
            pltpu.VMEM((2 * HALF, BLOCK), f32),
            pltpu.VMEM((R, R), f32),
            pltpu.VMEM((BLOCK, R), f32),
            pltpu.VMEM((BLOCK, R), bf16),
            pltpu.VMEM((8, 128), i32),
            pltpu.VMEM((3, 8, 128), i32),
            pltpu.VMEM((8, 128), i32),
            pltpu.VMEM((7, 8, 128), i32),
            dma((8,)),
            dma((8, 3)),
            dma((8, 3)),
            dma((2, 4)),
            dma((2, 4)),
            dma((3, 4)),
            dma((3, 4)),
            dma((10,)),
            dma((10,)),
            dma((30,)),
            dma((30,)),
            dma((2, 4)),
            dma((2, 4)),
            dma((8, 4)),
            dma((8, 4)),
            dma((3,)),
            dma((3,)),
            dma((2, 4, 2)),
            dma((2, 4, 2)),
        ],
        compiler_params=pltpu.CompilerParams(
            collective_id=0, has_side_effects=True, vmem_limit_bytes=48 * 1024 * 1024
        ),
        name="muon",
    )(grads.reshape(NZ, NX, BLOCK, R), momentum, weight, max_logits, threshold)
    return (new_master, new_momentum, new_weight.reshape(NZ * NX * BLOCK, R), blend_rms)


def solution(mesh):
    return jax.shard_map(
        local,
        mesh=mesh,
        in_specs=(
            P("dp", "col", None),
            P(("col", "dp"), None),
            P(("col", "dp"), None),
            P("dp", None, None),
            P(),
        ),
        out_specs=(P(("col", "dp"), None), P(("col", "dp"), None), P("col", None), P("col")),
        check_vma=False,
    )
```

```python
import functools

import jax
import jax.numpy as jnp
from jax import lax
from jax.experimental import pallas as pl
from jax.experimental.pallas import tpu as pltpu
from jax.sharding import PartitionSpec as P

R = 512
HEADS = 64
NOPE = 128
VDIM = 128
ITERS = 5
LAYERS = 2
F = 16384

NZ = 8
NX = 4
NY = 4
BLOCK = 128
CUT = 80
CA = 384
CB = R - CA
FINE = 2

momentum_rate = 0.95
epsilon = 1e-07
coef_one = 3.4445
coef_two = -4.775
coef_three = 2.0315
learn_rate = 0.02
decay_rate = 0.1

ORDER = (4, -3, 3, -2, 2, -1, 1, 0)
PAIRS = [(i, j) for i in range(4) for j in range(i, 4)]
HALF = len(PAIRS) * BLOCK // 2
PART = HALF // 8
SLAB = PART // 8


def exact(left, right, dims=((1,), (0,))):
    return lax.dot_general(
        left,
        right,
        (dims, ((), ())),
        precision=lax.Precision.HIGHEST,
        preferred_element_type=jnp.float32,
    )


def halves(value, count):
    terms = []
    for left in range(count, 0, -1):
        terms.append(value.astype(jnp.bfloat16))
        if left > 1:
            value = value - terms[-1].astype(jnp.float32)
    return terms


def split_product(left, right):
    def dot(i, j):
        return jnp.dot(left[i], right[j], preferred_element_type=jnp.float32)

    total = dot(0, 1) + dot(1, 0)
    if len(left) == 3:
        total = total + (dot(1, 1) + (dot(0, 2) + dot(2, 0)))
    return dot(0, 0) + total


def mirrored(left, right):
    half = R // 2
    top = split_product([term[0:half] for term in left], right)
    low = split_product([term[half:R] for term in left], [term[:, half:R] for term in right])
    return jnp.concatenate([top, jnp.concatenate([top[:, half:R].T, low], axis=1)], axis=0)


def kernel(
    grads,
    momentum,
    weight,
    max_logits,
    threshold,
    new_master,
    new_momentum,
    new_weight,
    blend_rms,
    own,
    own_b,
    rx,
    zs,
    zr,
    bs,
    br,
    b_raw,
    b_sum,
    b_in,
    moment_in,
    weight_in,
    moment_out,
    master_out,
    ml_in,
    packed,
    core_in,
    half_sum,
    xy_in,
    slab_out,
    slab_in,
    slab_sum,
    slab_all,
    full,
    gram,
    ortho,
    rounded,
    ml_out,
    ml_x,
    ml_mid,
    ml_z,
    s_local,
    s_x,
    r_x,
    s_z,
    r_z,
    s_b,
    r_b,
    s_ml,
    r_ml,
    s_g,
    r_g,
    s_az,
    r_az,
    s_ax,
    r_ax,
    s_bx,
    r_bx,
    s_bz,
    r_bz,
):
    d = lax.axis_index("dp")
    c = lax.axis_index("col")
    z, x = d // NX, d % NX
    y, core = c // 2, c % 2
    ybase = (y // 2) * 2
    xr, xl, xo = (x + 1) % NX, (x + 3) % NX, (x + 2) % NX
    zup, zdn = (z + 1) % NZ, (z + NZ - 1) % NZ
    m8 = x * 2 + y % 2

    def at_x(xx):
        return (z * NX + xx, c)

    def at_z(zz):
        return (zz * NX + x, c)

    def at_xy(p):
        return (z * NX + p // 2, (ybase + p % 2) * 2 + core)

    partner = (d, y * 2 + 1 - core)

    def send(src, dst, ss, rs, to):
        copy = pltpu.make_async_remote_copy(
            src_ref=src,
            dst_ref=dst,
            send_sem=ss,
            recv_sem=rs,
            device_id=to,
            device_id_type=pl.DeviceIdType.MESH,
        )
        copy.start()
        return copy

    sent = []

    def drain(copies):
        for copy in copies:
            copy.wait_send()
        del sent[: len(copies)]

    barrier = pltpu.get_barrier_semaphore()
    mates = [at_xy((m8 + r) % 8) for r in range(1, 8)]
    mates += [at_z((z + r) % NZ) for r in range(1, NZ)]
    mates += [partner]
    for mate in mates:
        pl.semaphore_signal(
            barrier, inc=1, device_id=mate, device_id_type=pl.DeviceIdType.MESH
        )
    loads = [
        pltpu.make_async_copy(grads.at[:, :, :, CA:R], own_b, s_local.at[0]),
        pltpu.make_async_copy(grads.at[:, x, :, 0:CA], own, s_local.at[1]),
        pltpu.make_async_copy(max_logits, ml_in, s_local.at[2]),
        pltpu.make_async_copy(momentum, moment_in, s_local.at[3]),
        pltpu.make_async_copy(weight, weight_in, s_local.at[4]),
    ]
    for copy in loads:
        copy.start()
    pl.semaphore_wait(barrier, len(mates))

    chunks = {}

    def start_chunk(j):
        zt = (z + ORDER[j] + NZ) % NZ
        chunks[j] = []
        for r in (1, 3, 2):
            xt = (x + r) % NX
            chunks[j].append(
                send(
                    grads.at[zt, xt, :, 0:CA],
                    rx.at[j, r - 1],
                    s_x.at[j, r - 1],
                    r_x.at[j, r - 1],
                    at_x(xt),
                )
            )
        sent.extend(chunks[j])

    ring = {}

    def finish_chunk(j):
        offset = ORDER[j]
        zt = (z + offset + NZ) % NZ
        for copy in chunks[j]:
            copy.wait_recv()
        value = own[zt].astype(jnp.float32) + rx[j, 0].astype(jnp.float32)
        value = value + (rx[j, 1].astype(jnp.float32) + rx[j, 2].astype(jnp.float32))
        if offset == 4:
            zs[0, 0, 0:64] = value[0:64]
            zs[1, 0, 0:64] = value[64:128]
            for way, to in ((0, zdn), (1, zup)):
                ring[way, 0] = send(
                    zs.at[way, 0, 0:64], zr.at[way, 0, 0:64], s_z.at[way, 0], r_z.at[way, 0], at_z(to)
                )
                sent.append(ring[way, 0])
        elif offset != 0:
            way = 0 if offset < 0 else 1
            to = zdn if offset < 0 else zup
            step = 4 - abs(offset)
            ring[way, step - 1].wait_recv()
            if step == 1:
                part = zr[way, 0, 0:64]
                zs[way, 1, 0:64] = value[0:64] + part if way == 0 else value[0:64]
                zs[way, 1, 64:128] = value[64:128] if way == 0 else value[64:128] + part
            else:
                zs[way, step] = value + zr[way, step - 1]
            ring[way, step] = send(
                zs.at[way, step], zr.at[way, step], s_z.at[way, step], r_z.at[way, step], at_z(to)
            )
            sent.append(ring[way, step])
        else:
            ring[0, 3].wait_recv()
            ring[1, 3].wait_recv()
            return value + (zr[0, 3] + zr[1, 3])

    wheel = {}

    def turn(step):
        for way, to in ((0, zdn), (1, zup)):
            sign = -1 if way == 0 else 1
            zt = (z + sign * (4 - step) + NZ) % NZ
            lo, up = 2 * way, 2 * way + 2
            if step == 0:
                src, dst = grads.at[zt, lo:up, :, CA:R], b_raw.at[way]
            else:
                wheel[way, step - 1].wait_recv()
                if step == 1:
                    rest = 2 - lo
                    bs[way, 1, lo:up] = own_b[zt, lo:up].astype(jnp.float32) + b_raw[way].astype(
                        jnp.float32
                    )
                    bs[way, 1, rest : rest + 2] = own_b[zt, rest : rest + 2].astype(jnp.float32)
                else:
                    bs[way, step] = own_b[zt].astype(jnp.float32) + br[way, step - 1]
                src, dst = bs.at[way, step], br.at[way, step]
            wheel[way, step] = send(src, dst, s_b.at[way, step], r_b.at[way, step], at_z(to))
            sent.append(wheel[way, step])

    turn(0)
    start_chunk(0)
    start_chunk(1)
    start_chunk(2)
    loads[2].wait()
    ml_out[...] = jnp.zeros_like(ml_out)
    ml_out[0:2, 0:HEADS] = ml_in[0]
    ml_sends = []
    for r in range(1, NX):
        ml_sends.append(
            send(ml_out, ml_x.at[r - 1], s_ml.at[r - 1], r_ml.at[r - 1], at_x((x + r) % NX))
        )
    sent.extend(ml_sends)
    loads[0].wait()
    turn(1)
    loads[1].wait()
    cross = []
    for j in range(7):
        finish_chunk(j)
        if j + 3 < 8:
            start_chunk(j + 3)
        if j in (0, 3):
            turn(2 if j == 0 else 3)
        if j == 3:
            for copy in ml_sends:
                copy.wait_recv()
            ml_mid[...] = jnp.maximum(
                jnp.maximum(ml_out[...], ml_x[0]), jnp.maximum(ml_x[1], ml_x[2])
            )
            ml_sends = []
            for r in range(1, NZ):
                ml_sends.append(
                    send(ml_mid, ml_z.at[r - 1], s_ml.at[r + 2], r_ml.at[r + 2], at_z((z + r) % NZ))
                )
            sent.extend(ml_sends)
        if j == 5:
            wheel[0, 3].wait_recv()
            wheel[1, 3].wait_recv()
            b_sum[...] = own_b[z].astype(jnp.float32) + (br[0, 3] + br[1, 3])
            for r in range(1, NX):
                xt = (x + r) % NX
                cross.append(
                    send(b_sum.at[xt], b_in.at[r - 1], s_b.at[2, r - 1], r_b.at[2, r - 1], at_x(xt))
                )
            sent.extend(cross)
    total_a = finish_chunk(7)
    loads[3].wait()
    loads[4].wait()
    total_b = b_sum[x]
    for r in range(1, NX):
        cross[r - 1].wait_recv()
        total_b = total_b + b_in[r - 1]

    for total, span in ((total_a, slice(0, CA)), (total_b, slice(CA, R))):
        mean_grad = total * (1.0 / (NZ * NX))
        moment = momentum_rate * moment_in[:, span] + mean_grad
        moment_out[:, span] = moment
        ortho[:, span] = mean_grad + momentum_rate * moment
    stores = [pltpu.make_async_copy(moment_out, new_momentum, s_local.at[5])]
    stores[0].start()

    low = 0
    for i in range(4):
        strip = exact(ortho[:, i * BLOCK : (i + 1) * BLOCK], ortho[:, i * BLOCK :], ((0,), (0,)))
        for j in range(i, 4):
            packed[low * BLOCK : (low + 1) * BLOCK] = strip[:, (j - i) * BLOCK : (j - i + 1) * BLOCK]
            low += 1
    def piece_of(which, p):
        return pl.ds(pl.multiple_of(which * HALF + p * PART, 8), PART)

    mates = [(m8 + r) % 8 for r in range(8)]
    swaps = []
    for r in (1, 2, 3, 4, 5, 6, 7, 0):
        p = mates[r]
        swaps.append(
            send(packed.at[piece_of(1 - core, p)], core_in.at[r], s_g.at[r], r_g.at[r], partner)
        )
    sent.extend(swaps)
    copies = []
    for r in range(1, 8):
        p = mates[r]
        swaps[r - 1].wait_recv()
        half_sum[r] = packed[piece_of(core, p)] + core_in[r]
        copies.append(send(half_sum.at[r], xy_in.at[r - 1], s_g.at[7 + r], r_g.at[7 + r], at_xy(p)))
    sent.extend(copies)
    swaps[7].wait_recv()
    part = packed[piece_of(core, m8)] + core_in[0]
    for r in range(1, 8):
        copies[r - 1].wait_recv()
        part = part + xy_in[r - 1]
    for i in range(8):
        slab_out[i] = part[i * SLAB : (i + 1) * SLAB]
    copies = []
    for r in range(1, NZ):
        zt = (z + r) % NZ
        copies.append(
            send(slab_out.at[zt], slab_in.at[r - 1], s_g.at[14 + r], r_g.at[14 + r], at_z(zt))
        )
    sent.extend(copies)
    drain(sent[:-7])
    slab = slab_out[z]
    for r in range(1, NZ):
        copies[r - 1].wait_recv()
        slab = slab + slab_in[r - 1]
    slab_sum[...] = slab
    slab_all[z] = slab
    copies = []
    for r in range(1, NZ):
        zt = (z + r) % NZ
        copies.append(
            send(slab_sum, slab_all.at[z], s_g.at[21 + r], r_g.at[21 + r], at_z(zt))
        )
    sent.extend(copies)
    for copy in copies:
        copy.wait_recv()
    here = piece_of(core, m8)
    full[here] = jnp.concatenate([slab_all[i] for i in range(8)], axis=0)
    copies = []
    for r in range(1, 8):
        copies.append(
            send(full.at[here], full.at[here], s_g.at[28 + r], r_g.at[28 + r], at_xy(mates[r]))
        )
    swaps = [send(full.at[here], full.at[here], s_g.at[36], r_g.at[36], partner)]
    for r in range(1, 8):
        copies[r - 1].wait_recv()
        there = piece_of(core, (m8 + 8 - r) % 8)
        swaps.append(send(full.at[there], full.at[there], s_g.at[36 + r], r_g.at[36 + r], partner))
    for copy in swaps:
        copy.wait_recv()
    sent.extend(copies)
    sent.extend(swaps)

    rows = lax.broadcasted_iota(jnp.int32, (BLOCK, BLOCK), 0)
    cols = lax.broadcasted_iota(jnp.int32, (BLOCK, BLOCK), 1)
    diagonal = jnp.zeros((BLOCK, BLOCK), jnp.float32)
    for low, (i, j) in enumerate(PAIRS):
        if i == j:
            block = full[low * BLOCK : (low + 1) * BLOCK]
            diagonal = diagonal + jnp.where(rows == cols, block, 0.0)
    square_total = jnp.sum(jnp.sum(diagonal, axis=0, keepdims=True), axis=1, keepdims=True)
    inverse = 1.0 / (jnp.sqrt(square_total) + epsilon)
    blend_rms[0] = jnp.sqrt(square_total * (1.0 / (F * R)))[0, 0]
    for low, (i, j) in enumerate(PAIRS):
        block = full[low * BLOCK : (low + 1) * BLOCK] * inverse * inverse
        gram[i * BLOCK : (i + 1) * BLOCK, j * BLOCK : (j + 1) * BLOCK] = block
        if i != j:
            gram[j * BLOCK : (j + 1) * BLOCK, i * BLOCK : (i + 1) * BLOCK] = block.T
    ortho[...] = ortho[...] * inverse

    def step(count, k, carry):
        now = halves(gram[...], count)
        square = mirrored(now[:2], now[:2])
        row_ids = lax.broadcasted_iota(jnp.int32, (R, R), 0)
        col_ids = lax.broadcasted_iota(jnp.int32, (R, R), 1)
        factor = halves(
            jnp.where(row_ids == col_ids, coef_one, 0.0) + coef_two * gram[...] + coef_three * square,
            count,
        )
        ortho[...] = split_product(halves(ortho[...], 2), factor[:2])
        if k is not None:
            once = halves(mirrored(now, factor), count)
            gram[...] = mirrored(once, factor)
        return carry

    lax.fori_loop(0, FINE, functools.partial(step, 3), 0)
    lax.fori_loop(FINE, ITERS - 1, functools.partial(step, 2), 0)
    step(2, None, 0)
    last = ortho[...]

    for copy in ml_sends:
        copy.wait_recv()
    peaks = ml_mid[...]
    for r in range(NZ - 1):
        peaks = jnp.maximum(peaks, ml_z[r])
    head = (c % (2 * NY // LAYERS)) * (HEADS * LAYERS // (2 * NY)) + d // 2
    layer = c // (2 * NY // LAYERS)
    rows = lax.broadcasted_iota(jnp.int32, (8, 128), 0)
    cols = lax.broadcasted_iota(jnp.int32, (8, 128), 1)
    chosen = jnp.where((rows == layer) & (cols == head), peaks, 0)
    peak = jnp.max(jnp.max(chosen, axis=0, keepdims=True), axis=1, keepdims=True)
    limit = jnp.full((1, 1), threshold[0], jnp.int32).astype(jnp.float32)
    gamma = jnp.minimum(1.0, limit / peak.astype(jnp.float32))
    scale = jnp.where(jnp.full((1, 1), d % 2, jnp.int32) == 0, jnp.sqrt(gamma), 1.0)
    update = last * (0.2 * float(max(F, R)) ** 0.5)
    stepped = weight_in[...] * (1.0 - learn_rate * decay_rate) - learn_rate * update
    master = stepped * scale
    master_out[...] = master
    stores.append(pltpu.make_async_copy(master_out, new_master, s_local.at[6]))
    rounded[...] = master.astype(jnp.bfloat16)

    stores.append(pltpu.make_async_copy(rounded, new_weight.at[z, x], s_local.at[7]))
    bx, az, ax, bz = [], {}, {}, {}
    for r in (1, 3, 2):
        bx.append(
            send(
                rounded.at[CUT:BLOCK],
                new_weight.at[z, x, CUT:BLOCK],
                s_bx.at[r - 1],
                r_bx.at[r - 1],
                at_x((x + r) % NX),
            )
        )

    def ring_a(step):
        up, down = (z + NZ - step) % NZ, (z + step) % NZ
        if step == 0:
            sources = [rounded.at[0:CUT], rounded.at[0:CUT]]
            spans = [(0, CUT), (0, CUT)]
        else:
            spans = [(0, CUT), (0, CUT)] if step < 3 else [(0, 48), (48, CUT)]
            sources = [
                new_weight.at[up, x, spans[0][0] : spans[0][1]],
                new_weight.at[down, x, spans[1][0] : spans[1][1]],
            ]
        for way, zz, to in ((0, up, zup), (1, down, zdn)):
            lo, hi = spans[way]
            az[way, step] = send(
                sources[way], new_weight.at[zz, x, lo:hi], s_az.at[way, step], r_az.at[way, step], at_z(to)
            )

    def ring_b(step):
        up, down = (z + NZ - step) % NZ, (z + step) % NZ
        for half in range(2):
            for way, zz, to in ((0, up, zup), (1, down, zdn)):
                if step > 0:
                    bz[way, step - 1, half].wait_recv()
                if step == 3 and half != way:
                    continue
                piece = new_weight.at[zz, 2 * half : 2 * half + 2, CUT:BLOCK]
                bz[way, step, half] = send(
                    piece, piece, s_bz.at[way, step, half], r_bz.at[way, step, half], at_z(to)
                )

    def spread(slot, zz, src):
        ax[slot] = [
            send(src, new_weight.at[zz, x, 0:CUT], s_ax.at[slot, 0], r_ax.at[slot, 0], at_x(xr)),
            send(src, new_weight.at[zz, x, 0:CUT], s_ax.at[slot, 1], r_ax.at[slot, 1], at_x(xl)),
        ]

    def spread_on(slot, zz):
        ax[slot][0].wait_recv()
        left = new_weight.at[zz, xl, 0:48]
        ax[slot].append(send(left, left, s_ax.at[slot, 2], r_ax.at[slot, 2], at_x(xr)))
        ax[slot][1].wait_recv()
        right = new_weight.at[zz, xr, 48:CUT]
        ax[slot].append(send(right, right, s_ax.at[slot, 3], r_ax.at[slot, 3], at_x(xl)))

    ring_a(0)
    spread(0, z, rounded.at[0:CUT])
    stores[1].start()
    stores[2].start()
    drain(sent[:])
    places = [z]
    for step in range(1, 5):
        az[0, step - 1].wait_recv()
        az[1, step - 1].wait_recv()
        up, down = (z + NZ - step) % NZ, (z + step) % NZ
        if step < 4:
            ring_a(step)
            spread(2 * step - 1, up, new_weight.at[up, x, 0:CUT])
            spread(2 * step, down, new_weight.at[down, x, 0:CUT])
            places.extend([up, down])
        else:
            spread(7, up, new_weight.at[up, x, 0:CUT])
            places.append(up)
        if step == 1:
            stores[2].wait()
            for copy in bx:
                copy.wait_recv()
        elif step == 2:
            spread_on(0, z)
        else:
            spread_on(2 * step - 5, places[2 * step - 5])
            spread_on(2 * step - 4, places[2 * step - 4])
        ring_b(step - 1)
    for slot in range(5, 8):
        spread_on(slot, places[slot])
    bz[0, 3, 0].wait_recv()
    bz[1, 3, 1].wait_recv()
    for slot in range(8):
        ax[slot][2].wait_recv()
        ax[slot][3].wait_recv()
    for copies in (bx, az.values(), bz.values(), *ax.values()):
        for copy in copies:
            copy.wait_send()
    stores[0].wait()
    stores[1].wait()


def local(grads, momentum, weight, max_logits, threshold):
    smem = pl.BlockSpec(memory_space=pltpu.SMEM)
    hbm = pl.BlockSpec(memory_space=pl.ANY)
    f32, bf16, i32 = jnp.float32, jnp.bfloat16, jnp.int32
    dma = pltpu.SemaphoreType.DMA
    new_master, new_momentum, new_weight, blend_rms = pl.pallas_call(
        kernel,
        out_shape=(
            jax.ShapeDtypeStruct((BLOCK, R), f32),
            jax.ShapeDtypeStruct((BLOCK, R), f32),
            jax.ShapeDtypeStruct((NZ, NX, BLOCK, R), bf16),
            jax.ShapeDtypeStruct((1,), f32),
        ),
        in_specs=[hbm, hbm, hbm, hbm, smem],
        out_specs=(hbm, hbm, hbm, smem),
        scratch_shapes=[
            pltpu.VMEM((NZ, BLOCK, CA), bf16),
            pltpu.VMEM((NZ, NX, BLOCK, CB), bf16),
            pltpu.VMEM((8, 3, BLOCK, CA), bf16),
            pltpu.VMEM((2, 4, BLOCK, CA), f32),
            pltpu.VMEM((2, 4, BLOCK, CA), f32),
            pltpu.VMEM((2, 4, NX, BLOCK, CB), f32),
            pltpu.VMEM((2, 4, NX, BLOCK, CB), f32),
            pltpu.VMEM((2, 2, BLOCK, CB), bf16),
            pltpu.VMEM((NX, BLOCK, CB), f32),
            pltpu.VMEM((3, BLOCK, CB), f32),
            pltpu.VMEM((BLOCK, R), f32),
            pltpu.VMEM((BLOCK, R), f32),
            pltpu.VMEM((BLOCK, R), f32),
            pltpu.VMEM((BLOCK, R), f32),
            pltpu.VMEM((1, LAYERS, HEADS), i32),
            pltpu.VMEM((2 * HALF, BLOCK), f32),
            pltpu.VMEM((8, PART, BLOCK), f32),
            pltpu.VMEM((8, PART, BLOCK), f32),
            pltpu.VMEM((7, PART, BLOCK), f32),
            pltpu.VMEM((8, SLAB, BLOCK), f32),
            pltpu.VMEM((7, SLAB, BLOCK), f32),
            pltpu.VMEM((SLAB, BLOCK), f32),
            pltpu.VMEM((8, SLAB, BLOCK), f32),
            pltpu.VMEM((2 * HALF, BLOCK), f32),
            pltpu.VMEM((R, R), f32),
            pltpu.VMEM((BLOCK, R), f32),
            pltpu.VMEM((BLOCK, R), bf16),
            pltpu.VMEM((8, 128), i32),
            pltpu.VMEM((3, 8, 128), i32),
            pltpu.VMEM((8, 128), i32),
            pltpu.VMEM((7, 8, 128), i32),
            dma((8,)),
            dma((8, 3)),
            dma((8, 3)),
            dma((2, 4)),
            dma((2, 4)),
            dma((3, 4)),
            dma((3, 4)),
            dma((10,)),
            dma((10,)),
            dma((44,)),
            dma((44,)),
            dma((2, 4)),
            dma((2, 4)),
            dma((8, 4)),
            dma((8, 4)),
            dma((3,)),
            dma((3,)),
            dma((2, 4, 2)),
            dma((2, 4, 2)),
        ],
        compiler_params=pltpu.CompilerParams(
            collective_id=0, has_side_effects=True, vmem_limit_bytes=48 * 1024 * 1024
        ),
        name="muon",
    )(grads.reshape(NZ, NX, BLOCK, R), momentum, weight, max_logits, threshold)
    return (new_master, new_momentum, new_weight.reshape(NZ * NX * BLOCK, R), blend_rms)


def solution(mesh):
    return jax.shard_map(
        local,
        mesh=mesh,
        in_specs=(
            P("dp", "col", None),
            P(("col", "dp"), None),
            P(("col", "dp"), None),
            P("dp", None, None),
            P(),
        ),
        out_specs=(P(("col", "dp"), None), P(("col", "dp"), None), P("col", None), P("col")),
        check_vma=False,
    )
```

```python
import functools

import jax
import jax.numpy as jnp
from jax import lax
from jax.experimental import pallas as pl
from jax.experimental.pallas import tpu as pltpu
from jax.sharding import PartitionSpec as P

R = 512
HEADS = 64
NOPE = 128
VDIM = 128
ITERS = 5
LAYERS = 2
F = 16384

NZ = 8
NX = 4
NY = 4
BLOCK = 128
CUT = 80
CA = 384
CB = R - CA
FINE = 2

momentum_rate = 0.95
epsilon = 1e-07
coef_one = 3.4445
coef_two = -4.775
coef_three = 2.0315
learn_rate = 0.02
decay_rate = 0.1

ORDER = (4, -3, 3, -2, 2, -1, 1, 0)
PAIRS = [(i, j) for i in range(4) for j in range(i, 4)]
HALF = len(PAIRS) * BLOCK // 2
PART = HALF // 16


def exact(left, right, dims=((1,), (0,))):
    return lax.dot_general(
        left,
        right,
        (dims, ((), ())),
        precision=lax.Precision.HIGHEST,
        preferred_element_type=jnp.float32,
    )


def halves(value, count):
    terms = []
    for left in range(count, 0, -1):
        terms.append(value.astype(jnp.bfloat16))
        if left > 1:
            value = value - terms[-1].astype(jnp.float32)
    return terms


def split_product(left, right):
    def dot(i, j):
        return jnp.dot(left[i], right[j], preferred_element_type=jnp.float32)

    total = dot(0, 1) + dot(1, 0)
    if len(left) == 3:
        total = total + (dot(1, 1) + (dot(0, 2) + dot(2, 0)))
    return dot(0, 0) + total


def mirrored(left, right):
    half = R // 2
    top = split_product([term[0:half] for term in left], right)
    low = split_product([term[half:R] for term in left], [term[:, half:R] for term in right])
    return jnp.concatenate([top, jnp.concatenate([top[:, half:R].T, low], axis=1)], axis=0)


def kernel(
    grads,
    momentum,
    weight,
    max_logits,
    threshold,
    new_master,
    new_momentum,
    new_weight,
    blend_rms,
    own,
    own_b,
    rx,
    zs,
    zr,
    bs,
    br,
    b_raw,
    b_sum,
    b_in,
    moment_in,
    weight_in,
    moment_out,
    master_out,
    ml_in,
    packed,
    core_in,
    half_sum,
    group_in,
    mid,
    row_in,
    full,
    gram,
    ortho,
    rounded,
    ml_out,
    ml_x,
    ml_mid,
    ml_pair,
    ml_z,
    s_local,
    s_x,
    r_x,
    s_z,
    r_z,
    s_b,
    r_b,
    s_ml,
    r_ml,
    s_g,
    r_g,
    s_az,
    r_az,
    s_ax,
    r_ax,
    s_bx,
    r_bx,
    s_bz,
    r_bz,
):
    d = lax.axis_index("dp")
    c = lax.axis_index("col")
    z, x = d // NX, d % NX
    y, core = c // 2, c % 2
    ybase = (y // 2) * 2
    xr, xl, xo = (x + 1) % NX, (x + 3) % NX, (x + 2) % NX
    zup, zdn = (z + 1) % NZ, (z + NZ - 1) % NZ
    m16 = (x * 2 + y % 2) * 2 + z % 2
    zpair = (z // 2) * 2

    def at_x(xx):
        return (z * NX + xx, c)

    def at_z(zz):
        return (zz * NX + x, c)

    def at_group(p):
        return ((zpair + p % 2) * NX + p // 4, (ybase + (p // 2) % 2) * 2 + core)

    partner = (d, y * 2 + 1 - core)

    def send(src, dst, ss, rs, to):
        copy = pltpu.make_async_remote_copy(
            src_ref=src,
            dst_ref=dst,
            send_sem=ss,
            recv_sem=rs,
            device_id=to,
            device_id_type=pl.DeviceIdType.MESH,
        )
        copy.start()
        return copy

    sent = []

    def drain(copies):
        for copy in copies:
            copy.wait_send()
        del sent[: len(copies)]

    barrier = pltpu.get_barrier_semaphore()
    mates = [at_group((m16 + r) % 16) for r in range(1, 16)]
    mates += [at_z((z + r) % NZ) for r in (2, 4, 6)]
    mates += [at_z((z + 7 - 6 * (z % 2)) % NZ), partner]
    for mate in mates:
        pl.semaphore_signal(
            barrier, inc=1, device_id=mate, device_id_type=pl.DeviceIdType.MESH
        )
    loads = [
        pltpu.make_async_copy(grads.at[:, :, :, CA:R], own_b, s_local.at[0]),
        pltpu.make_async_copy(grads.at[:, x, :, 0:CA], own, s_local.at[1]),
        pltpu.make_async_copy(max_logits, ml_in, s_local.at[2]),
        pltpu.make_async_copy(momentum, moment_in, s_local.at[3]),
        pltpu.make_async_copy(weight, weight_in, s_local.at[4]),
    ]
    for copy in loads:
        copy.start()
    pl.semaphore_wait(barrier, len(mates))

    chunks = {}

    def start_chunk(j):
        zt = (z + ORDER[j] + NZ) % NZ
        chunks[j] = []
        for r in (1, 3, 2):
            xt = (x + r) % NX
            chunks[j].append(
                send(
                    grads.at[zt, xt, :, 0:CA],
                    rx.at[j, r - 1],
                    s_x.at[j, r - 1],
                    r_x.at[j, r - 1],
                    at_x(xt),
                )
            )
        sent.extend(chunks[j])

    ring = {}

    def finish_chunk(j):
        offset = ORDER[j]
        zt = (z + offset + NZ) % NZ
        for copy in chunks[j]:
            copy.wait_recv()
        value = own[zt].astype(jnp.float32) + rx[j, 0].astype(jnp.float32)
        value = value + (rx[j, 1].astype(jnp.float32) + rx[j, 2].astype(jnp.float32))
        if offset == 4:
            zs[0, 0, 0:64] = value[0:64]
            zs[1, 0, 0:64] = value[64:128]
            for way, to in ((0, zdn), (1, zup)):
                ring[way, 0] = send(
                    zs.at[way, 0, 0:64], zr.at[way, 0, 0:64], s_z.at[way, 0], r_z.at[way, 0], at_z(to)
                )
                sent.append(ring[way, 0])
        elif offset != 0:
            way = 0 if offset < 0 else 1
            to = zdn if offset < 0 else zup
            step = 4 - abs(offset)
            ring[way, step - 1].wait_recv()
            if step == 1:
                part = zr[way, 0, 0:64]
                zs[way, 1, 0:64] = value[0:64] + part if way == 0 else value[0:64]
                zs[way, 1, 64:128] = value[64:128] if way == 0 else value[64:128] + part
            else:
                zs[way, step] = value + zr[way, step - 1]
            ring[way, step] = send(
                zs.at[way, step], zr.at[way, step], s_z.at[way, step], r_z.at[way, step], at_z(to)
            )
            sent.append(ring[way, step])
        else:
            ring[0, 3].wait_recv()
            ring[1, 3].wait_recv()
            return value + (zr[0, 3] + zr[1, 3])

    wheel = {}

    def turn(step):
        for way, to in ((0, zdn), (1, zup)):
            sign = -1 if way == 0 else 1
            zt = (z + sign * (4 - step) + NZ) % NZ
            lo, up = 2 * way, 2 * way + 2
            if step == 0:
                src, dst = grads.at[zt, lo:up, :, CA:R], b_raw.at[way]
            else:
                wheel[way, step - 1].wait_recv()
                if step == 1:
                    rest = 2 - lo
                    bs[way, 1, lo:up] = own_b[zt, lo:up].astype(jnp.float32) + b_raw[way].astype(
                        jnp.float32
                    )
                    bs[way, 1, rest : rest + 2] = own_b[zt, rest : rest + 2].astype(jnp.float32)
                else:
                    bs[way, step] = own_b[zt].astype(jnp.float32) + br[way, step - 1]
                src, dst = bs.at[way, step], br.at[way, step]
            wheel[way, step] = send(src, dst, s_b.at[way, step], r_b.at[way, step], at_z(to))
            sent.append(wheel[way, step])

    turn(0)
    start_chunk(0)
    start_chunk(1)
    start_chunk(2)
    loads[2].wait()
    ml_out[...] = jnp.zeros_like(ml_out)
    ml_out[0:2, 0:HEADS] = ml_in[0]
    ml_sends = []
    for r in range(1, NX):
        ml_sends.append(
            send(ml_out, ml_x.at[r - 1], s_ml.at[r - 1], r_ml.at[r - 1], at_x((x + r) % NX))
        )
    sent.extend(ml_sends)
    loads[0].wait()
    turn(1)
    loads[1].wait()
    cross = []
    for j in range(7):
        finish_chunk(j)
        if j + 3 < 8:
            start_chunk(j + 3)
        if j in (0, 3):
            turn(2 if j == 0 else 3)
        if j == 3:
            for copy in ml_sends:
                copy.wait_recv()
            ml_mid[...] = jnp.maximum(
                jnp.maximum(ml_out[...], ml_x[0]), jnp.maximum(ml_x[1], ml_x[2])
            )
            ml_sends = [send(ml_mid, ml_z.at[0], s_ml.at[3], r_ml.at[3], at_z(zpair + 1 - z % 2))]
            sent.extend(ml_sends)
        if j == 5:
            wheel[0, 3].wait_recv()
            wheel[1, 3].wait_recv()
            b_sum[...] = own_b[z].astype(jnp.float32) + (br[0, 3] + br[1, 3])
            for r in range(1, NX):
                xt = (x + r) % NX
                cross.append(
                    send(b_sum.at[xt], b_in.at[r - 1], s_b.at[2, r - 1], r_b.at[2, r - 1], at_x(xt))
                )
            sent.extend(cross)
            ml_sends[0].wait_recv()
            ml_pair[...] = jnp.maximum(ml_mid[...], ml_z[0])
            ml_sends = []
            for k in range(1, 4):
                ml_sends.append(
                    send(ml_pair, ml_z.at[k], s_ml.at[3 + k], r_ml.at[3 + k], at_z((z + 2 * k) % NZ))
                )
            sent.extend(ml_sends)
    total_a = finish_chunk(7)
    loads[3].wait()
    loads[4].wait()
    total_b = b_sum[x]
    for r in range(1, NX):
        cross[r - 1].wait_recv()
        total_b = total_b + b_in[r - 1]

    for total, span in ((total_a, slice(0, CA)), (total_b, slice(CA, R))):
        mean_grad = total * (1.0 / (NZ * NX))
        moment = momentum_rate * moment_in[:, span] + mean_grad
        moment_out[:, span] = moment
        ortho[:, span] = mean_grad + momentum_rate * moment
    stores = [pltpu.make_async_copy(moment_out, new_momentum, s_local.at[5])]
    stores[0].start()

    low = 0
    for i in range(4):
        strip = exact(ortho[:, i * BLOCK : (i + 1) * BLOCK], ortho[:, i * BLOCK :], ((0,), (0,)))
        for j in range(i, 4):
            packed[low * BLOCK : (low + 1) * BLOCK] = strip[:, (j - i) * BLOCK : (j - i + 1) * BLOCK]
            low += 1

    def piece_of(which, p):
        return pl.ds(pl.multiple_of(which * HALF + p * PART, 8), PART)

    mine = pl.ds(pl.multiple_of(core * HALF, 8), HALF)
    theirs = pl.ds(pl.multiple_of((1 - core) * HALF, 8), HALF)
    swap = send(packed.at[theirs], core_in, s_g.at[0], r_g.at[0], partner)
    swap.wait_recv()
    half_sum[...] = packed[mine] + core_in[...]
    copies = []
    for r in range(1, 16):
        p = (m16 + r) % 16
        copies.append(
            send(half_sum.at[piece_of(0, p)], group_in.at[r - 1], s_g.at[r], r_g.at[r], at_group(p))
        )
    drain(sent[:])
    sent.extend([swap] + copies)
    part = half_sum[piece_of(0, m16)]
    for r in range(1, 16):
        copies[r - 1].wait_recv()
        part = part + group_in[r - 1]
    mid[...] = part
    row_in[z // 2] = part
    copies = []
    for k in range(1, 4):
        copies.append(
            send(mid, row_in.at[z // 2], s_g.at[15 + k], r_g.at[15 + k], at_z((z + 2 * k) % NZ))
        )
    for copy in copies:
        copy.wait_recv()
    sent.extend(copies)
    here = piece_of(core, m16)
    full[here] = (row_in[0] + row_in[1]) + (row_in[2] + row_in[3])
    copies = []
    for r in range(1, 16):
        copies.append(
            send(
                full.at[here], full.at[here], s_g.at[18 + r], r_g.at[18 + r], at_group((m16 + r) % 16)
            )
        )
    swaps = [send(full.at[here], full.at[here], s_g.at[34], r_g.at[34], partner)]
    for r in range(1, 16):
        copies[r - 1].wait_recv()
        there = piece_of(core, (m16 + 16 - r) % 16)
        swaps.append(send(full.at[there], full.at[there], s_g.at[34 + r], r_g.at[34 + r], partner))
    for copy in swaps:
        copy.wait_recv()
    sent.extend(copies)
    sent.extend(swaps)

    rows = lax.broadcasted_iota(jnp.int32, (BLOCK, BLOCK), 0)
    cols = lax.broadcasted_iota(jnp.int32, (BLOCK, BLOCK), 1)
    diagonal = jnp.zeros((BLOCK, BLOCK), jnp.float32)
    for low, (i, j) in enumerate(PAIRS):
        if i == j:
            block = full[low * BLOCK : (low + 1) * BLOCK]
            diagonal = diagonal + jnp.where(rows == cols, block, 0.0)
    square_total = jnp.sum(jnp.sum(diagonal, axis=0, keepdims=True), axis=1, keepdims=True)
    inverse = 1.0 / (jnp.sqrt(square_total) + epsilon)
    blend_rms[0] = jnp.sqrt(square_total * (1.0 / (F * R)))[0, 0]
    for low, (i, j) in enumerate(PAIRS):
        block = full[low * BLOCK : (low + 1) * BLOCK] * inverse * inverse
        gram[i * BLOCK : (i + 1) * BLOCK, j * BLOCK : (j + 1) * BLOCK] = block
        if i != j:
            gram[j * BLOCK : (j + 1) * BLOCK, i * BLOCK : (i + 1) * BLOCK] = block.T
    ortho[...] = ortho[...] * inverse

    def step(count, k, carry):
        now = halves(gram[...], count)
        square = mirrored(now[:2], now[:2])
        row_ids = lax.broadcasted_iota(jnp.int32, (R, R), 0)
        col_ids = lax.broadcasted_iota(jnp.int32, (R, R), 1)
        factor = halves(
            jnp.where(row_ids == col_ids, coef_one, 0.0) + coef_two * gram[...] + coef_three * square,
            count,
        )
        ortho[...] = split_product(halves(ortho[...], 2), factor[:2])
        if k is not None:
            once = halves(mirrored(now, factor), count)
            gram[...] = mirrored(once, factor)
        return carry

    lax.fori_loop(0, FINE, functools.partial(step, 3), 0)
    lax.fori_loop(FINE, ITERS - 1, functools.partial(step, 2), 0)
    step(2, None, 0)
    last = ortho[...]

    for copy in ml_sends:
        copy.wait_recv()
    peaks = ml_pair[...]
    for k in range(1, 4):
        peaks = jnp.maximum(peaks, ml_z[k])
    head = (c % (2 * NY // LAYERS)) * (HEADS * LAYERS // (2 * NY)) + d // 2
    layer = c // (2 * NY // LAYERS)
    rows = lax.broadcasted_iota(jnp.int32, (8, 128), 0)
    cols = lax.broadcasted_iota(jnp.int32, (8, 128), 1)
    chosen = jnp.where((rows == layer) & (cols == head), peaks, 0)
    peak = jnp.max(jnp.max(chosen, axis=0, keepdims=True), axis=1, keepdims=True)
    limit = jnp.full((1, 1), threshold[0], jnp.int32).astype(jnp.float32)
    gamma = jnp.minimum(1.0, limit / peak.astype(jnp.float32))
    scale = jnp.where(jnp.full((1, 1), d % 2, jnp.int32) == 0, jnp.sqrt(gamma), 1.0)
    update = last * (0.2 * float(max(F, R)) ** 0.5)
    stepped = weight_in[...] * (1.0 - learn_rate * decay_rate) - learn_rate * update
    master = stepped * scale
    master_out[...] = master
    stores.append(pltpu.make_async_copy(master_out, new_master, s_local.at[6]))
    rounded[...] = master.astype(jnp.bfloat16)

    stores.append(pltpu.make_async_copy(rounded, new_weight.at[z, x], s_local.at[7]))
    bx, az, ax, bz = [], {}, {}, {}
    for r in (1, 3, 2):
        bx.append(
            send(
                rounded.at[CUT:BLOCK],
                new_weight.at[z, x, CUT:BLOCK],
                s_bx.at[r - 1],
                r_bx.at[r - 1],
                at_x((x + r) % NX),
            )
        )

    def first_a(distance):
        for way, to in ((0, (z + distance) % NZ), (1, (z + NZ - distance) % NZ)):
            az[way, distance] = send(
                rounded.at[0:CUT],
                new_weight.at[z, x, 0:CUT],
                s_az.at[way, distance - 1],
                r_az.at[way, distance - 1],
                at_z(to),
            )

    def ring_a(distance):
        for way, zz, to in (
            (0, (z + NZ - distance + 1) % NZ, zup),
            (1, (z + distance - 1) % NZ, zdn),
        ):
            lo, hi = (0, CUT) if distance < 4 else ((0, 48) if way == 0 else (48, CUT))
            piece = new_weight.at[zz, x, lo:hi]
            az[way, distance] = send(
                piece, piece, s_az.at[way, distance - 1], r_az.at[way, distance - 1], at_z(to)
            )

    def ring_b(step, r):
        xx = (x + r) % NX
        for way, zz, to in ((0, (z + NZ - step) % NZ, zup), (1, (z + step) % NZ, zdn)):
            if step > 0:
                bz[way, step - 1, r].wait_recv()
            if step == 3 and (r < 2) != (way == 0):
                continue
            piece = new_weight.at[zz, xx, CUT:BLOCK]
            src = rounded.at[CUT:BLOCK] if step == 0 and r == 0 else piece
            bz[way, step, r] = send(
                src, piece, s_bz.at[way, step, r], r_bz.at[way, step, r], at_z(to)
            )

    def spread(slot, zz, src):
        ax[slot] = [
            send(src, new_weight.at[zz, x, 0:CUT], s_ax.at[slot, 0], r_ax.at[slot, 0], at_x(xr)),
            send(src, new_weight.at[zz, x, 0:CUT], s_ax.at[slot, 1], r_ax.at[slot, 1], at_x(xl)),
        ]

    def spread_on(slot, zz):
        ax[slot][0].wait_recv()
        left = new_weight.at[zz, xl, 0:48]
        ax[slot].append(send(left, left, s_ax.at[slot, 2], r_ax.at[slot, 2], at_x(xr)))
        ax[slot][1].wait_recv()
        right = new_weight.at[zz, xr, 48:CUT]
        ax[slot].append(send(right, right, s_ax.at[slot, 3], r_ax.at[slot, 3], at_x(xl)))

    first_a(1)
    first_a(2)
    spread(0, z, rounded.at[0:CUT])
    ring_b(0, 0)
    stores[1].start()
    stores[2].start()
    drain(sent[:])
    places = [z]
    for k in range(1, 4):
        places.extend([(z + NZ - k) % NZ, (z + k) % NZ])
    places.append((z + 4) % NZ)

    def arrived(distance):
        az[0, distance].wait_recv()
        az[1, distance].wait_recv()

    def spread_two(k):
        for slot in (2 * k - 1, 2 * k):
            spread(slot, places[slot], new_weight.at[places[slot], x, 0:CUT])

    arrived(1)
    spread_two(1)
    arrived(2)
    ring_a(3)
    spread_two(2)
    for r in (1, 3, 2):
        bx[(3, 1, 2).index(r)].wait_recv()
        ring_b(0, r)
    spread_on(0, z)
    ring_b(1, 0)
    arrived(3)
    ring_a(4)
    spread_two(3)
    spread_on(1, places[1])
    spread_on(2, places[2])
    for r in (1, 3, 2):
        ring_b(1, r)
    arrived(4)
    spread(7, places[7], new_weight.at[places[7], x, 0:CUT])
    spread_on(3, places[3])
    spread_on(4, places[4])
    for r in (0, 1, 3, 2):
        ring_b(2, r)
    spread_on(5, places[5])
    spread_on(6, places[6])
    for r in (0, 1, 3, 2):
        ring_b(3, r)
    spread_on(7, places[7])
    for r in range(4):
        bz[r // 2, 3, r].wait_recv()
    stores[2].wait()
    for slot in range(8):
        ax[slot][2].wait_recv()
        ax[slot][3].wait_recv()
    for copies in (bx, az.values(), bz.values(), *ax.values()):
        for copy in copies:
            copy.wait_send()
    stores[0].wait()
    stores[1].wait()


def local(grads, momentum, weight, max_logits, threshold):
    smem = pl.BlockSpec(memory_space=pltpu.SMEM)
    hbm = pl.BlockSpec(memory_space=pl.ANY)
    f32, bf16, i32 = jnp.float32, jnp.bfloat16, jnp.int32
    dma = pltpu.SemaphoreType.DMA
    new_master, new_momentum, new_weight, blend_rms = pl.pallas_call(
        kernel,
        out_shape=(
            jax.ShapeDtypeStruct((BLOCK, R), f32),
            jax.ShapeDtypeStruct((BLOCK, R), f32),
            jax.ShapeDtypeStruct((NZ, NX, BLOCK, R), bf16),
            jax.ShapeDtypeStruct((1,), f32),
        ),
        in_specs=[hbm, hbm, hbm, hbm, smem],
        out_specs=(hbm, hbm, hbm, smem),
        scratch_shapes=[
            pltpu.VMEM((NZ, BLOCK, CA), bf16),
            pltpu.VMEM((NZ, NX, BLOCK, CB), bf16),
            pltpu.VMEM((8, 3, BLOCK, CA), bf16),
            pltpu.VMEM((2, 4, BLOCK, CA), f32),
            pltpu.VMEM((2, 4, BLOCK, CA), f32),
            pltpu.VMEM((2, 4, NX, BLOCK, CB), f32),
            pltpu.VMEM((2, 4, NX, BLOCK, CB), f32),
            pltpu.VMEM((2, 2, BLOCK, CB), bf16),
            pltpu.VMEM((NX, BLOCK, CB), f32),
            pltpu.VMEM((3, BLOCK, CB), f32),
            pltpu.VMEM((BLOCK, R), f32),
            pltpu.VMEM((BLOCK, R), f32),
            pltpu.VMEM((BLOCK, R), f32),
            pltpu.VMEM((BLOCK, R), f32),
            pltpu.VMEM((1, LAYERS, HEADS), i32),
            pltpu.VMEM((2 * HALF, BLOCK), f32),
            pltpu.VMEM((HALF, BLOCK), f32),
            pltpu.VMEM((HALF, BLOCK), f32),
            pltpu.VMEM((15, PART, BLOCK), f32),
            pltpu.VMEM((PART, BLOCK), f32),
            pltpu.VMEM((4, PART, BLOCK), f32),
            pltpu.VMEM((2 * HALF, BLOCK), f32),
            pltpu.VMEM((R, R), f32),
            pltpu.VMEM((BLOCK, R), f32),
            pltpu.VMEM((BLOCK, R), bf16),
            pltpu.VMEM((8, 128), i32),
            pltpu.VMEM((3, 8, 128), i32),
            pltpu.VMEM((8, 128), i32),
            pltpu.VMEM((8, 128), i32),
            pltpu.VMEM((4, 8, 128), i32),
            dma((8,)),
            dma((8, 3)),
            dma((8, 3)),
            dma((2, 4)),
            dma((2, 4)),
            dma((3, 4)),
            dma((3, 4)),
            dma((10,)),
            dma((10,)),
            dma((50,)),
            dma((50,)),
            dma((2, 4)),
            dma((2, 4)),
            dma((8, 4)),
            dma((8, 4)),
            dma((3,)),
            dma((3,)),
            dma((2, 4, 4)),
            dma((2, 4, 4)),
        ],
        compiler_params=pltpu.CompilerParams(
            collective_id=0, has_side_effects=True, vmem_limit_bytes=48 * 1024 * 1024
        ),
        name="muon",
    )(grads.reshape(NZ, NX, BLOCK, R), momentum, weight, max_logits, threshold)
    return (new_master, new_momentum, new_weight.reshape(NZ * NX * BLOCK, R), blend_rms)


def solution(mesh):
    return jax.shard_map(
        local,
        mesh=mesh,
        in_specs=(
            P("dp", "col", None),
            P(("col", "dp"), None),
            P(("col", "dp"), None),
            P("dp", None, None),
            P(),
        ),
        out_specs=(P(("col", "dp"), None), P(("col", "dp"), None), P("col", None), P("col")),
        check_vma=False,
    )
```

```python
import functools

import jax
import jax.numpy as jnp
from jax import lax
from jax.experimental import pallas as pl
from jax.experimental.pallas import tpu as pltpu
from jax.sharding import PartitionSpec as P

R = 512
HEADS = 64
NOPE = 128
VDIM = 128
ITERS = 5
LAYERS = 2
F = 16384

NZ = 8
NX = 4
NY = 4
BLOCK = 128
CUT = 80
CA = 384
CB = R - CA
FINE = 2

momentum_rate = 0.95
epsilon = 1e-07
coef_one = 3.4445
coef_two = -4.775
coef_three = 2.0315
learn_rate = 0.02
decay_rate = 0.1

ORDER = (4, -3, 3, -2, 2, -1, 1, 0)
PAIRS = [(i, j) for i in range(4) for j in range(i, 4)]
HALF = len(PAIRS) * BLOCK // 2
PART = HALF // 16


def exact(left, right, dims=((1,), (0,))):
    return lax.dot_general(
        left,
        right,
        (dims, ((), ())),
        precision=lax.Precision.HIGHEST,
        preferred_element_type=jnp.float32,
    )


def halves(value, count):
    terms = []
    for left in range(count, 0, -1):
        terms.append(value.astype(jnp.bfloat16))
        if left > 1:
            value = value - terms[-1].astype(jnp.float32)
    return terms


def split_product(left, right):
    def dot(i, j):
        return jnp.dot(left[i], right[j], preferred_element_type=jnp.float32)

    total = dot(0, 1) + dot(1, 0)
    if len(left) == 3:
        total = total + (dot(1, 1) + (dot(0, 2) + dot(2, 0)))
    return dot(0, 0) + total


def mirrored(left, right):
    half = R // 2
    top = split_product([term[0:half] for term in left], right)
    low = split_product([term[half:R] for term in left], [term[:, half:R] for term in right])
    return jnp.concatenate([top, jnp.concatenate([top[:, half:R].T, low], axis=1)], axis=0)


def kernel(
    grads,
    momentum,
    weight,
    max_logits,
    threshold,
    new_master,
    new_momentum,
    new_weight,
    blend_rms,
    own,
    own_b,
    rx,
    zs,
    zr,
    bs,
    br,
    b_raw,
    b_sum,
    b_in,
    moment_in,
    weight_in,
    moment_out,
    master_out,
    ml_in,
    packed,
    core_in,
    half_sum,
    group_in,
    mid,
    row_in,
    full,
    gram,
    ortho,
    rounded,
    ml_out,
    ml_x,
    ml_mid,
    ml_pair,
    ml_z,
    plane,
    s_local,
    s_x,
    r_x,
    s_z,
    r_z,
    s_b,
    r_b,
    s_ml,
    r_ml,
    s_g,
    r_g,
    s_az,
    r_az,
    s_ax,
    r_ax,
    s_bx,
    r_bx,
    s_bz,
    r_bz,
):
    d = lax.axis_index("dp")
    c = lax.axis_index("col")
    z, x = d // NX, d % NX
    y, core = c // 2, c % 2
    ybase = (y // 2) * 2
    xr, xl, xo = (x + 1) % NX, (x + 3) % NX, (x + 2) % NX
    zup, zdn = (z + 1) % NZ, (z + NZ - 1) % NZ
    m16 = (x * 2 + y % 2) * 2 + z % 2
    zpair = (z // 2) * 2

    def at_x(xx):
        return (z * NX + xx, c)

    def at_z(zz):
        return (zz * NX + x, c)

    def at_group(p):
        return ((zpair + p % 2) * NX + p // 4, (ybase + (p // 2) % 2) * 2 + core)

    partner = (d, y * 2 + 1 - core)

    def send(src, dst, ss, rs, to):
        copy = pltpu.make_async_remote_copy(
            src_ref=src,
            dst_ref=dst,
            send_sem=ss,
            recv_sem=rs,
            device_id=to,
            device_id_type=pl.DeviceIdType.MESH,
        )
        copy.start()
        return copy

    sent = []

    def drain(copies):
        for copy in copies:
            copy.wait_send()
        del sent[: len(copies)]

    barrier = pltpu.get_barrier_semaphore()
    across = (d, (ybase + 1 - y % 2) * 2 + core)
    mates = [at_x(xr), at_x(xl), at_x(xo), at_z(zup), at_z(zdn), across, partner]
    for mate in mates:
        pl.semaphore_signal(
            barrier, inc=1, device_id=mate, device_id_type=pl.DeviceIdType.MESH
        )
    loads = [
        pltpu.make_async_copy(grads.at[:, :, :, CA:R], own_b, s_local.at[0]),
        pltpu.make_async_copy(grads.at[:, x, :, 0:CA], own, s_local.at[1]),
        pltpu.make_async_copy(max_logits, ml_in, s_local.at[2]),
        pltpu.make_async_copy(momentum, moment_in, s_local.at[3]),
        pltpu.make_async_copy(weight, weight_in, s_local.at[4]),
    ]
    for copy in loads:
        copy.start()
    pl.semaphore_wait(barrier, len(mates))

    chunks = {}

    def start_chunk(j):
        zt = (z + ORDER[j] + NZ) % NZ
        chunks[j] = []
        for r in (1, 3, 2):
            xt = (x + r) % NX
            chunks[j].append(
                send(
                    grads.at[zt, xt, :, 0:CA],
                    rx.at[j, r - 1],
                    s_x.at[j, r - 1],
                    r_x.at[j, r - 1],
                    at_x(xt),
                )
            )
        sent.extend(chunks[j])

    ring = {}

    def finish_chunk(j):
        offset = ORDER[j]
        zt = (z + offset + NZ) % NZ
        for copy in chunks[j]:
            copy.wait_recv()
        value = own[zt].astype(jnp.float32) + rx[j, 0].astype(jnp.float32)
        value = value + (rx[j, 1].astype(jnp.float32) + rx[j, 2].astype(jnp.float32))
        if offset == 4:
            zs[0, 0, 0:64] = value[0:64]
            zs[1, 0, 0:64] = value[64:128]
            for way, to in ((0, zdn), (1, zup)):
                ring[way, 0] = send(
                    zs.at[way, 0, 0:64], zr.at[way, 0, 0:64], s_z.at[way, 0], r_z.at[way, 0], at_z(to)
                )
                sent.append(ring[way, 0])
        elif offset != 0:
            way = 0 if offset < 0 else 1
            to = zdn if offset < 0 else zup
            step = 4 - abs(offset)
            ring[way, step - 1].wait_recv()
            if step == 1:
                part = zr[way, 0, 0:64]
                zs[way, 1, 0:64] = value[0:64] + part if way == 0 else value[0:64]
                zs[way, 1, 64:128] = value[64:128] if way == 0 else value[64:128] + part
            else:
                zs[way, step] = value + zr[way, step - 1]
            ring[way, step] = send(
                zs.at[way, step], zr.at[way, step], s_z.at[way, step], r_z.at[way, step], at_z(to)
            )
            sent.append(ring[way, step])
        else:
            ring[0, 3].wait_recv()
            ring[1, 3].wait_recv()
            return value + (zr[0, 3] + zr[1, 3])

    wheel = {}

    def turn(step):
        for way, to in ((0, zdn), (1, zup)):
            sign = -1 if way == 0 else 1
            zt = (z + sign * (4 - step) + NZ) % NZ
            lo, up = 2 * way, 2 * way + 2
            if step == 0:
                src, dst = grads.at[zt, lo:up, :, CA:R], b_raw.at[way]
            else:
                wheel[way, step - 1].wait_recv()
                if step == 1:
                    rest = 2 - lo
                    bs[way, 1, lo:up] = own_b[zt, lo:up].astype(jnp.float32) + b_raw[way].astype(
                        jnp.float32
                    )
                    bs[way, 1, rest : rest + 2] = own_b[zt, rest : rest + 2].astype(jnp.float32)
                else:
                    bs[way, step] = own_b[zt].astype(jnp.float32) + br[way, step - 1]
                src, dst = bs.at[way, step], br.at[way, step]
            wheel[way, step] = send(src, dst, s_b.at[way, step], r_b.at[way, step], at_z(to))
            sent.append(wheel[way, step])

    turn(0)
    start_chunk(0)
    start_chunk(1)
    start_chunk(2)
    loads[2].wait()
    ml_out[...] = jnp.zeros_like(ml_out)
    ml_out[0:2, 0:HEADS] = ml_in[0]
    ml_sends = []
    for r in range(1, NX):
        ml_sends.append(
            send(ml_out, ml_x.at[r - 1], s_ml.at[r - 1], r_ml.at[r - 1], at_x((x + r) % NX))
        )
    sent.extend(ml_sends)
    loads[0].wait()
    turn(1)
    loads[1].wait()
    cross = []
    for j in range(7):
        finish_chunk(j)
        if j + 3 < 8:
            start_chunk(j + 3)
        if j in (0, 3):
            turn(2 if j == 0 else 3)
        if j == 3:
            for copy in ml_sends:
                copy.wait_recv()
            ml_mid[...] = jnp.maximum(
                jnp.maximum(ml_out[...], ml_x[0]), jnp.maximum(ml_x[1], ml_x[2])
            )
            ml_sends = [send(ml_mid, ml_z.at[0], s_ml.at[3], r_ml.at[3], at_z(zpair + 1 - z % 2))]
            sent.extend(ml_sends)
        if j == 4:
            pl.semaphore_signal(
                plane, inc=1, device_id=across, device_id_type=pl.DeviceIdType.MESH
            )
        if j == 5:
            wheel[0, 3].wait_recv()
            wheel[1, 3].wait_recv()
            b_sum[...] = own_b[z].astype(jnp.float32) + (br[0, 3] + br[1, 3])
            for r in range(1, NX):
                xt = (x + r) % NX
                cross.append(
                    send(b_sum.at[xt], b_in.at[r - 1], s_b.at[2, r - 1], r_b.at[2, r - 1], at_x(xt))
                )
            sent.extend(cross)
            ml_sends[0].wait_recv()
            ml_pair[...] = jnp.maximum(ml_mid[...], ml_z[0])
            ml_sends = []
            for k in range(1, 4):
                ml_sends.append(
                    send(ml_pair, ml_z.at[k], s_ml.at[3 + k], r_ml.at[3 + k], at_z((z + 2 * k) % NZ))
                )
            sent.extend(ml_sends)
    total_a = finish_chunk(7)
    loads[3].wait()
    loads[4].wait()
    total_b = b_sum[x]
    for r in range(1, NX):
        cross[r - 1].wait_recv()
        total_b = total_b + b_in[r - 1]

    for total, span in ((total_a, slice(0, CA)), (total_b, slice(CA, R))):
        mean_grad = total * (1.0 / (NZ * NX))
        moment = momentum_rate * moment_in[:, span] + mean_grad
        moment_out[:, span] = moment
        ortho[:, span] = mean_grad + momentum_rate * moment
    stores = [pltpu.make_async_copy(moment_out, new_momentum, s_local.at[5])]
    stores[0].start()

    low = 0
    for i in range(4):
        strip = exact(ortho[:, i * BLOCK : (i + 1) * BLOCK], ortho[:, i * BLOCK :], ((0,), (0,)))
        for j in range(i, 4):
            packed[low * BLOCK : (low + 1) * BLOCK] = strip[:, (j - i) * BLOCK : (j - i + 1) * BLOCK]
            low += 1

    def piece_of(which, p):
        return pl.ds(pl.multiple_of(which * HALF + p * PART, 8), PART)

    mine = pl.ds(pl.multiple_of(core * HALF, 8), HALF)
    theirs = pl.ds(pl.multiple_of((1 - core) * HALF, 8), HALF)
    swap = send(packed.at[theirs], core_in, s_g.at[0], r_g.at[0], partner)
    swap.wait_recv()
    half_sum[...] = packed[mine] + core_in[...]
    pl.semaphore_wait(plane, 1)
    copies = []
    for r in range(1, 16):
        p = (m16 + r) % 16
        copies.append(
            send(half_sum.at[piece_of(0, p)], group_in.at[r - 1], s_g.at[r], r_g.at[r], at_group(p))
        )
    drain(sent[:])
    sent.extend([swap] + copies)
    part = half_sum[piece_of(0, m16)]
    for r in range(1, 16):
        copies[r - 1].wait_recv()
        part = part + group_in[r - 1]
    mid[...] = part
    row_in[z // 2] = part
    copies = []
    for k in range(1, 4):
        copies.append(
            send(mid, row_in.at[z // 2], s_g.at[15 + k], r_g.at[15 + k], at_z((z + 2 * k) % NZ))
        )
    for copy in copies:
        copy.wait_recv()
    sent.extend(copies)
    here = piece_of(core, m16)
    full[here] = (row_in[0] + row_in[1]) + (row_in[2] + row_in[3])
    copies = []
    for r in range(1, 16):
        copies.append(
            send(
                full.at[here], full.at[here], s_g.at[18 + r], r_g.at[18 + r], at_group((m16 + r) % 16)
            )
        )
    swaps = [send(full.at[here], full.at[here], s_g.at[34], r_g.at[34], partner)]
    for r in range(1, 16):
        copies[r - 1].wait_recv()
        there = piece_of(core, (m16 + 16 - r) % 16)
        swaps.append(send(full.at[there], full.at[there], s_g.at[34 + r], r_g.at[34 + r], partner))
    for copy in swaps:
        copy.wait_recv()
    sent.extend(copies)
    sent.extend(swaps)

    rows = lax.broadcasted_iota(jnp.int32, (BLOCK, BLOCK), 0)
    cols = lax.broadcasted_iota(jnp.int32, (BLOCK, BLOCK), 1)
    diagonal = jnp.zeros((BLOCK, BLOCK), jnp.float32)
    for low, (i, j) in enumerate(PAIRS):
        if i == j:
            block = full[low * BLOCK : (low + 1) * BLOCK]
            diagonal = diagonal + jnp.where(rows == cols, block, 0.0)
    square_total = jnp.sum(jnp.sum(diagonal, axis=0, keepdims=True), axis=1, keepdims=True)
    inverse = 1.0 / (jnp.sqrt(square_total) + epsilon)
    blend_rms[0] = jnp.sqrt(square_total * (1.0 / (F * R)))[0, 0]
    for low, (i, j) in enumerate(PAIRS):
        block = full[low * BLOCK : (low + 1) * BLOCK] * inverse * inverse
        gram[i * BLOCK : (i + 1) * BLOCK, j * BLOCK : (j + 1) * BLOCK] = block
        if i != j:
            gram[j * BLOCK : (j + 1) * BLOCK, i * BLOCK : (i + 1) * BLOCK] = block.T
    ortho[...] = ortho[...] * inverse

    def step(count, k, carry):
        now = halves(gram[...], count)
        square = mirrored(now[:2], now[:2])
        row_ids = lax.broadcasted_iota(jnp.int32, (R, R), 0)
        col_ids = lax.broadcasted_iota(jnp.int32, (R, R), 1)
        factor = halves(
            jnp.where(row_ids == col_ids, coef_one, 0.0) + coef_two * gram[...] + coef_three * square,
            count,
        )
        ortho[...] = split_product(halves(ortho[...], 2), factor[:2])
        once = halves(mirrored(now, factor), count)
        gram[...] = mirrored(once, factor)
        return carry

    lax.fori_loop(0, FINE, functools.partial(step, 3), 0)
    lax.fori_loop(FINE, ITERS - 1, functools.partial(step, 2), 0)
    now = halves(gram[...], 2)
    first = ortho[...]
    second = split_product(halves(first, 2), now)
    third = split_product(halves(second, 2), now)
    last = coef_one * first + coef_two * second + coef_three * third

    for copy in ml_sends:
        copy.wait_recv()
    peaks = ml_pair[...]
    for k in range(1, 4):
        peaks = jnp.maximum(peaks, ml_z[k])
    head = (c % (2 * NY // LAYERS)) * (HEADS * LAYERS // (2 * NY)) + d // 2
    layer = c // (2 * NY // LAYERS)
    rows = lax.broadcasted_iota(jnp.int32, (8, 128), 0)
    cols = lax.broadcasted_iota(jnp.int32, (8, 128), 1)
    chosen = jnp.where((rows == layer) & (cols == head), peaks, 0)
    peak = jnp.max(jnp.max(chosen, axis=0, keepdims=True), axis=1, keepdims=True)
    limit = jnp.full((1, 1), threshold[0], jnp.int32).astype(jnp.float32)
    gamma = jnp.minimum(1.0, limit / peak.astype(jnp.float32))
    scale = jnp.where(jnp.full((1, 1), d % 2, jnp.int32) == 0, jnp.sqrt(gamma), 1.0)
    update = last * (0.2 * float(max(F, R)) ** 0.5)
    stepped = weight_in[...] * (1.0 - learn_rate * decay_rate) - learn_rate * update
    master = stepped * scale
    master_out[...] = master
    stores.append(pltpu.make_async_copy(master_out, new_master, s_local.at[6]))
    rounded[...] = master.astype(jnp.bfloat16)

    stores.append(pltpu.make_async_copy(rounded, new_weight.at[z, x], s_local.at[7]))
    bx, az, ax, bz = [], {}, {}, {}
    for r in (1, 3, 2):
        bx.append(
            send(
                rounded.at[CUT:BLOCK],
                new_weight.at[z, x, CUT:BLOCK],
                s_bx.at[r - 1],
                r_bx.at[r - 1],
                at_x((x + r) % NX),
            )
        )

    def first_a(distance):
        for way, to in ((0, (z + distance) % NZ), (1, (z + NZ - distance) % NZ)):
            az[way, distance] = send(
                rounded.at[0:CUT],
                new_weight.at[z, x, 0:CUT],
                s_az.at[way, distance - 1],
                r_az.at[way, distance - 1],
                at_z(to),
            )

    def ring_a(distance):
        for way, zz, to in (
            (0, (z + NZ - distance + 1) % NZ, zup),
            (1, (z + distance - 1) % NZ, zdn),
        ):
            lo, hi = (0, CUT) if distance < 4 else ((0, 48) if way == 0 else (48, CUT))
            piece = new_weight.at[zz, x, lo:hi]
            az[way, distance] = send(
                piece, piece, s_az.at[way, distance - 1], r_az.at[way, distance - 1], at_z(to)
            )

    def ring_b(step, r):
        xx = (x + r) % NX
        for way, zz, to in ((0, (z + NZ - step) % NZ, zup), (1, (z + step) % NZ, zdn)):
            if step > 0:
                bz[way, step - 1, r].wait_recv()
            if step == 3 and (r < 2) != (way == 0):
                continue
            piece = new_weight.at[zz, xx, CUT:BLOCK]
            src = rounded.at[CUT:BLOCK] if step == 0 and r == 0 else piece
            bz[way, step, r] = send(
                src, piece, s_bz.at[way, step, r], r_bz.at[way, step, r], at_z(to)
            )

    def spread(slot, zz, src):
        ax[slot] = [
            send(src, new_weight.at[zz, x, 0:CUT], s_ax.at[slot, 0], r_ax.at[slot, 0], at_x(xr)),
            send(src, new_weight.at[zz, x, 0:CUT], s_ax.at[slot, 1], r_ax.at[slot, 1], at_x(xl)),
        ]

    def spread_on(slot, zz):
        ax[slot][0].wait_recv()
        left = new_weight.at[zz, xl, 0:48]
        ax[slot].append(send(left, left, s_ax.at[slot, 2], r_ax.at[slot, 2], at_x(xr)))
        ax[slot][1].wait_recv()
        right = new_weight.at[zz, xr, 48:CUT]
        ax[slot].append(send(right, right, s_ax.at[slot, 3], r_ax.at[slot, 3], at_x(xl)))

    first_a(1)
    first_a(2)
    spread(0, z, rounded.at[0:CUT])
    ring_b(0, 0)
    stores[1].start()
    stores[2].start()
    drain(sent[:])
    places = [z]
    for k in range(1, 4):
        places.extend([(z + NZ - k) % NZ, (z + k) % NZ])
    places.append((z + 4) % NZ)

    def arrived(distance):
        az[0, distance].wait_recv()
        az[1, distance].wait_recv()

    def spread_two(k):
        for slot in (2 * k - 1, 2 * k):
            spread(slot, places[slot], new_weight.at[places[slot], x, 0:CUT])

    arrived(1)
    spread_two(1)
    arrived(2)
    ring_a(3)
    spread_two(2)
    for r in (1, 3, 2):
        bx[(3, 1, 2).index(r)].wait_recv()
        ring_b(0, r)
    spread_on(0, z)
    ring_b(1, 0)
    arrived(3)
    ring_a(4)
    spread_two(3)
    spread_on(1, places[1])
    spread_on(2, places[2])
    for r in (1, 3, 2):
        ring_b(1, r)
    arrived(4)
    spread(7, places[7], new_weight.at[places[7], x, 0:CUT])
    spread_on(3, places[3])
    spread_on(4, places[4])
    for r in (0, 1, 3, 2):
        ring_b(2, r)
    spread_on(5, places[5])
    spread_on(6, places[6])
    for r in (0, 1, 3, 2):
        ring_b(3, r)
    spread_on(7, places[7])
    for r in range(4):
        bz[r // 2, 3, r].wait_recv()
    stores[2].wait()
    for slot in range(8):
        ax[slot][2].wait_recv()
        ax[slot][3].wait_recv()
    for copies in (bx, az.values(), bz.values(), *ax.values()):
        for copy in copies:
            copy.wait_send()
    stores[0].wait()
    stores[1].wait()


def local(grads, momentum, weight, max_logits, threshold):
    smem = pl.BlockSpec(memory_space=pltpu.SMEM)
    hbm = pl.BlockSpec(memory_space=pl.ANY)
    f32, bf16, i32 = jnp.float32, jnp.bfloat16, jnp.int32
    dma = pltpu.SemaphoreType.DMA
    new_master, new_momentum, new_weight, blend_rms = pl.pallas_call(
        kernel,
        out_shape=(
            jax.ShapeDtypeStruct((BLOCK, R), f32),
            jax.ShapeDtypeStruct((BLOCK, R), f32),
            jax.ShapeDtypeStruct((NZ, NX, BLOCK, R), bf16),
            jax.ShapeDtypeStruct((1,), f32),
        ),
        in_specs=[hbm, hbm, hbm, hbm, smem],
        out_specs=(hbm, hbm, hbm, smem),
        scratch_shapes=[
            pltpu.VMEM((NZ, BLOCK, CA), bf16),
            pltpu.VMEM((NZ, NX, BLOCK, CB), bf16),
            pltpu.VMEM((8, 3, BLOCK, CA), bf16),
            pltpu.VMEM((2, 4, BLOCK, CA), f32),
            pltpu.VMEM((2, 4, BLOCK, CA), f32),
            pltpu.VMEM((2, 4, NX, BLOCK, CB), f32),
            pltpu.VMEM((2, 4, NX, BLOCK, CB), f32),
            pltpu.VMEM((2, 2, BLOCK, CB), bf16),
            pltpu.VMEM((NX, BLOCK, CB), f32),
            pltpu.VMEM((3, BLOCK, CB), f32),
            pltpu.VMEM((BLOCK, R), f32),
            pltpu.VMEM((BLOCK, R), f32),
            pltpu.VMEM((BLOCK, R), f32),
            pltpu.VMEM((BLOCK, R), f32),
            pltpu.VMEM((1, LAYERS, HEADS), i32),
            pltpu.VMEM((2 * HALF, BLOCK), f32),
            pltpu.VMEM((HALF, BLOCK), f32),
            pltpu.VMEM((HALF, BLOCK), f32),
            pltpu.VMEM((15, PART, BLOCK), f32),
            pltpu.VMEM((PART, BLOCK), f32),
            pltpu.VMEM((4, PART, BLOCK), f32),
            pltpu.VMEM((2 * HALF, BLOCK), f32),
            pltpu.VMEM((R, R), f32),
            pltpu.VMEM((BLOCK, R), f32),
            pltpu.VMEM((BLOCK, R), bf16),
            pltpu.VMEM((8, 128), i32),
            pltpu.VMEM((3, 8, 128), i32),
            pltpu.VMEM((8, 128), i32),
            pltpu.VMEM((8, 128), i32),
            pltpu.VMEM((4, 8, 128), i32),
            pltpu.SemaphoreType.REGULAR,
            dma((8,)),
            dma((8, 3)),
            dma((8, 3)),
            dma((2, 4)),
            dma((2, 4)),
            dma((3, 4)),
            dma((3, 4)),
            dma((10,)),
            dma((10,)),
            dma((50,)),
            dma((50,)),
            dma((2, 4)),
            dma((2, 4)),
            dma((8, 4)),
            dma((8, 4)),
            dma((3,)),
            dma((3,)),
            dma((2, 4, 4)),
            dma((2, 4, 4)),
        ],
        compiler_params=pltpu.CompilerParams(
            collective_id=0, has_side_effects=True, vmem_limit_bytes=48 * 1024 * 1024
        ),
        name="muon",
    )(grads.reshape(NZ, NX, BLOCK, R), momentum, weight, max_logits, threshold)
    return (new_master, new_momentum, new_weight.reshape(NZ * NX * BLOCK, R), blend_rms)


def solution(mesh):
    return jax.shard_map(
        local,
        mesh=mesh,
        in_specs=(
            P("dp", "col", None),
            P(("col", "dp"), None),
            P(("col", "dp"), None),
            P("dp", None, None),
            P(),
        ),
        out_specs=(P(("col", "dp"), None), P(("col", "dp"), None), P("col", None), P("col")),
        check_vma=False,
    )
```

```python
import functools

import jax
import jax.numpy as jnp
from jax import lax
from jax.experimental import pallas as pl
from jax.experimental.pallas import tpu as pltpu
from jax.sharding import PartitionSpec as P

R = 512
HEADS = 64
NOPE = 128
VDIM = 128
ITERS = 5
LAYERS = 2
F = 16384

NZ = 8
NX = 4
NY = 4
BLOCK = 128
CUT = 80
CA = 384
CB = R - CA
FINE = 2

momentum_rate = 0.95
epsilon = 1e-07
coef_one = 3.4445
coef_two = -4.775
coef_three = 2.0315
learn_rate = 0.02
decay_rate = 0.1

ORDER = (4, -3, 3, -2, 2, -1, 1, 0)
PAIRS = [(i, j) for i in range(4) for j in range(i, 4)]
HALF = len(PAIRS) * BLOCK // 2
PART = HALF // 16


def exact(left, right, dims=((1,), (0,))):
    return lax.dot_general(
        left,
        right,
        (dims, ((), ())),
        precision=lax.Precision.HIGHEST,
        preferred_element_type=jnp.float32,
    )


def halves(value, count):
    terms = []
    for left in range(count, 0, -1):
        terms.append(value.astype(jnp.bfloat16))
        if left > 1:
            value = value - terms[-1].astype(jnp.float32)
    return terms


def split_product(left, right):
    def dot(i, j):
        return jnp.dot(left[i], right[j], preferred_element_type=jnp.float32)

    total = dot(0, 1) + dot(1, 0)
    if len(left) == 3:
        total = total + (dot(1, 1) + (dot(0, 2) + dot(2, 0)))
    return dot(0, 0) + total


def mirrored(left, right):
    half = R // 2
    top = split_product([term[0:half] for term in left], right)
    low = split_product([term[half:R] for term in left], [term[:, half:R] for term in right])
    return jnp.concatenate([top, jnp.concatenate([top[:, half:R].T, low], axis=1)], axis=0)


def kernel(
    grads,
    momentum,
    weight,
    max_logits,
    threshold,
    new_master,
    new_momentum,
    new_weight,
    blend_rms,
    own,
    own_b,
    rx,
    zs,
    zr,
    bs,
    br,
    b_raw,
    b_sum,
    b_in,
    moment_in,
    weight_in,
    moment_out,
    master_out,
    ml_in,
    packed,
    core_in,
    half_sum,
    group_in,
    mid,
    row_in,
    full,
    gram,
    ortho,
    rounded,
    ml_out,
    ml_x,
    ml_mid,
    ml_pair,
    scale_out,
    ml_z,
    plane,
    s_local,
    s_x,
    r_x,
    s_z,
    r_z,
    s_b,
    r_b,
    s_ml,
    r_ml,
    s_g,
    r_g,
    s_az,
    r_az,
    s_ax,
    r_ax,
    s_bx,
    r_bx,
    s_bz,
    r_bz,
):
    d = lax.axis_index("dp")
    c = lax.axis_index("col")
    z, x = d // NX, d % NX
    y, core = c // 2, c % 2
    ybase = (y // 2) * 2
    xr, xl, xo = (x + 1) % NX, (x + 3) % NX, (x + 2) % NX
    zup, zdn = (z + 1) % NZ, (z + NZ - 1) % NZ
    m16 = (x * 2 + y % 2) * 2 + z % 2
    zpair = (z // 2) * 2

    def at_x(xx):
        return (z * NX + xx, c)

    def at_z(zz):
        return (zz * NX + x, c)

    def at_group(p):
        return ((zpair + p % 2) * NX + p // 4, (ybase + (p // 2) % 2) * 2 + core)

    partner = (d, y * 2 + 1 - core)

    def send(src, dst, ss, rs, to):
        copy = pltpu.make_async_remote_copy(
            src_ref=src,
            dst_ref=dst,
            send_sem=ss,
            recv_sem=rs,
            device_id=to,
            device_id_type=pl.DeviceIdType.MESH,
        )
        copy.start()
        return copy

    sent = []

    def drain(copies):
        for copy in copies:
            copy.wait_send()
        del sent[: len(copies)]

    barrier = pltpu.get_barrier_semaphore()
    across = (d, (ybase + 1 - y % 2) * 2 + core)
    mates = [at_x(xr), at_x(xl), at_x(xo), at_z(zup), at_z(zdn), across, partner]
    for mate in mates:
        pl.semaphore_signal(
            barrier, inc=1, device_id=mate, device_id_type=pl.DeviceIdType.MESH
        )
    loads = [
        pltpu.make_async_copy(grads.at[:, :, :, CA:R], own_b, s_local.at[0]),
        pltpu.make_async_copy(grads.at[:, x, :, 0:CA], own, s_local.at[1]),
        pltpu.make_async_copy(max_logits, ml_in, s_local.at[2]),
        pltpu.make_async_copy(momentum, moment_in, s_local.at[3]),
        pltpu.make_async_copy(weight, weight_in, s_local.at[4]),
    ]
    for copy in loads:
        copy.start()
    pl.semaphore_wait(barrier, len(mates))

    chunks = {}

    def start_chunk(j):
        zt = (z + ORDER[j] + NZ) % NZ
        chunks[j] = []
        for r in (1, 3, 2):
            xt = (x + r) % NX
            chunks[j].append(
                send(
                    grads.at[zt, xt, :, 0:CA],
                    rx.at[j, r - 1],
                    s_x.at[j, r - 1],
                    r_x.at[j, r - 1],
                    at_x(xt),
                )
            )
        sent.extend(chunks[j])

    ring = {}

    def finish_chunk(j):
        offset = ORDER[j]
        zt = (z + offset + NZ) % NZ
        for copy in chunks[j]:
            copy.wait_recv()
        value = own[zt].astype(jnp.float32) + rx[j, 0].astype(jnp.float32)
        value = value + (rx[j, 1].astype(jnp.float32) + rx[j, 2].astype(jnp.float32))
        if offset == 4:
            zs[0, 0, 0:64] = value[0:64]
            zs[1, 0, 0:64] = value[64:128]
            for way, to in ((0, zdn), (1, zup)):
                ring[way, 0] = send(
                    zs.at[way, 0, 0:64], zr.at[way, 0, 0:64], s_z.at[way, 0], r_z.at[way, 0], at_z(to)
                )
                sent.append(ring[way, 0])
        elif offset != 0:
            way = 0 if offset < 0 else 1
            to = zdn if offset < 0 else zup
            step = 4 - abs(offset)
            ring[way, step - 1].wait_recv()
            if step == 1:
                part = zr[way, 0, 0:64]
                zs[way, 1, 0:64] = value[0:64] + part if way == 0 else value[0:64]
                zs[way, 1, 64:128] = value[64:128] if way == 0 else value[64:128] + part
            else:
                zs[way, step] = value + zr[way, step - 1]
            ring[way, step] = send(
                zs.at[way, step], zr.at[way, step], s_z.at[way, step], r_z.at[way, step], at_z(to)
            )
            sent.append(ring[way, step])
        else:
            ring[0, 3].wait_recv()
            ring[1, 3].wait_recv()
            return value + (zr[0, 3] + zr[1, 3])

    wheel = {}

    def turn(step):
        for way, to in ((0, zdn), (1, zup)):
            sign = -1 if way == 0 else 1
            zt = (z + sign * (4 - step) + NZ) % NZ
            lo, up = 2 * way, 2 * way + 2
            if step == 0:
                src, dst = grads.at[zt, lo:up, :, CA:R], b_raw.at[way]
            else:
                wheel[way, step - 1].wait_recv()
                if step == 1:
                    rest = 2 - lo
                    bs[way, 1, lo:up] = own_b[zt, lo:up].astype(jnp.float32) + b_raw[way].astype(
                        jnp.float32
                    )
                    bs[way, 1, rest : rest + 2] = own_b[zt, rest : rest + 2].astype(jnp.float32)
                else:
                    bs[way, step] = own_b[zt].astype(jnp.float32) + br[way, step - 1]
                src, dst = bs.at[way, step], br.at[way, step]
            wheel[way, step] = send(src, dst, s_b.at[way, step], r_b.at[way, step], at_z(to))
            sent.append(wheel[way, step])

    turn(0)
    start_chunk(0)
    start_chunk(1)
    start_chunk(2)
    loads[2].wait()
    ml_out[...] = jnp.zeros_like(ml_out)
    ml_out[0:2, 0:HEADS] = ml_in[0]
    ml_sends = []
    for r in range(1, NX):
        ml_sends.append(
            send(ml_out, ml_x.at[r - 1], s_ml.at[r - 1], r_ml.at[r - 1], at_x((x + r) % NX))
        )
    sent.extend(ml_sends)
    loads[0].wait()
    turn(1)
    loads[1].wait()
    cross = []
    for j in range(7):
        finish_chunk(j)
        if j + 3 < 8:
            start_chunk(j + 3)
        if j in (0, 3):
            turn(2 if j == 0 else 3)
        if j == 3:
            for copy in ml_sends:
                copy.wait_recv()
            ml_mid[...] = jnp.maximum(
                jnp.maximum(ml_out[...], ml_x[0]), jnp.maximum(ml_x[1], ml_x[2])
            )
            ml_sends = [send(ml_mid, ml_z.at[0], s_ml.at[3], r_ml.at[3], at_z(zpair + 1 - z % 2))]
            sent.extend(ml_sends)
        if j == 4:
            pl.semaphore_signal(
                plane, inc=1, device_id=across, device_id_type=pl.DeviceIdType.MESH
            )
        if j == 5:
            wheel[0, 3].wait_recv()
            wheel[1, 3].wait_recv()
            b_sum[...] = own_b[z].astype(jnp.float32) + (br[0, 3] + br[1, 3])
            for r in range(1, NX):
                xt = (x + r) % NX
                cross.append(
                    send(b_sum.at[xt], b_in.at[r - 1], s_b.at[2, r - 1], r_b.at[2, r - 1], at_x(xt))
                )
            sent.extend(cross)
            ml_sends[0].wait_recv()
            ml_pair[...] = jnp.maximum(ml_mid[...], ml_z[0])
            ml_sends = []
            for k in range(1, 4):
                ml_sends.append(
                    send(ml_pair, ml_z.at[k], s_ml.at[3 + k], r_ml.at[3 + k], at_z((z + 2 * k) % NZ))
                )
            sent.extend(ml_sends)
    total_a = finish_chunk(7)
    loads[3].wait()
    loads[4].wait()
    total_b = b_sum[x]
    for r in range(1, NX):
        cross[r - 1].wait_recv()
        total_b = total_b + b_in[r - 1]

    for total, span in ((total_a, slice(0, CA)), (total_b, slice(CA, R))):
        mean_grad = total * (1.0 / (NZ * NX))
        moment = momentum_rate * moment_in[:, span] + mean_grad
        moment_out[:, span] = moment
        ortho[:, span] = mean_grad + momentum_rate * moment
    stores = [pltpu.make_async_copy(moment_out, new_momentum, s_local.at[5])]
    stores[0].start()

    low = 0
    for i in range(4):
        strip = exact(ortho[:, i * BLOCK : (i + 1) * BLOCK], ortho[:, i * BLOCK :], ((0,), (0,)))
        for j in range(i, 4):
            packed[low * BLOCK : (low + 1) * BLOCK] = strip[:, (j - i) * BLOCK : (j - i + 1) * BLOCK]
            low += 1

    def piece_of(which, p):
        return pl.ds(pl.multiple_of(which * HALF + p * PART, 8), PART)

    mine = pl.ds(pl.multiple_of(core * HALF, 8), HALF)
    theirs = pl.ds(pl.multiple_of((1 - core) * HALF, 8), HALF)
    swap = send(packed.at[theirs], core_in, s_g.at[0], r_g.at[0], partner)
    swap.wait_recv()
    half_sum[...] = packed[mine] + core_in[...]
    pl.semaphore_wait(plane, 1)
    copies = []
    for r in range(1, 16):
        p = (m16 + r) % 16
        copies.append(
            send(half_sum.at[piece_of(0, p)], group_in.at[r - 1], s_g.at[r], r_g.at[r], at_group(p))
        )
    drain(sent[:])
    sent.extend([swap] + copies)
    for copy in ml_sends:
        copy.wait_recv()
    peaks = ml_pair[...]
    for k in range(1, 4):
        peaks = jnp.maximum(peaks, ml_z[k])
    head = (c % (2 * NY // LAYERS)) * (HEADS * LAYERS // (2 * NY)) + d // 2
    layer = c // (2 * NY // LAYERS)
    rows = lax.broadcasted_iota(jnp.int32, (8, 128), 0)
    cols = lax.broadcasted_iota(jnp.int32, (8, 128), 1)
    chosen = jnp.where((rows == layer) & (cols == head), peaks, 0)
    peak = jnp.max(jnp.max(chosen, axis=0, keepdims=True), axis=1, keepdims=True)
    limit = jnp.full((1, 1), threshold[0], jnp.int32).astype(jnp.float32)
    gamma = jnp.minimum(1.0, limit / peak.astype(jnp.float32))
    scale = jnp.where(jnp.full((1, 1), d % 2, jnp.int32) == 0, jnp.sqrt(gamma), 1.0)
    scale_out[...] = jnp.broadcast_to(scale, (8, 128))
    part = half_sum[piece_of(0, m16)]
    for r in range(1, 16):
        copies[r - 1].wait_recv()
        part = part + group_in[r - 1]
    mid[...] = part
    row_in[z // 2] = part
    copies = []
    for k in range(1, 4):
        copies.append(
            send(mid, row_in.at[z // 2], s_g.at[15 + k], r_g.at[15 + k], at_z((z + 2 * k) % NZ))
        )
    for copy in copies:
        copy.wait_recv()
    sent.extend(copies)
    here = piece_of(core, m16)
    full[here] = (row_in[0] + row_in[1]) + (row_in[2] + row_in[3])
    copies = []
    for r in range(1, 16):
        copies.append(
            send(
                full.at[here], full.at[here], s_g.at[18 + r], r_g.at[18 + r], at_group((m16 + r) % 16)
            )
        )
    swaps = [send(full.at[here], full.at[here], s_g.at[34], r_g.at[34], partner)]
    for r in range(1, 16):
        copies[r - 1].wait_recv()
        there = piece_of(core, (m16 + 16 - r) % 16)
        swaps.append(send(full.at[there], full.at[there], s_g.at[34 + r], r_g.at[34 + r], partner))
    for copy in swaps:
        copy.wait_recv()
    sent.extend(copies)
    sent.extend(swaps)

    rows = lax.broadcasted_iota(jnp.int32, (BLOCK, BLOCK), 0)
    cols = lax.broadcasted_iota(jnp.int32, (BLOCK, BLOCK), 1)
    diagonal = jnp.zeros((BLOCK, BLOCK), jnp.float32)
    for low, (i, j) in enumerate(PAIRS):
        if i == j:
            block = full[low * BLOCK : (low + 1) * BLOCK]
            diagonal = diagonal + jnp.where(rows == cols, block, 0.0)
    square_total = jnp.sum(jnp.sum(diagonal, axis=0, keepdims=True), axis=1, keepdims=True)
    inverse = 1.0 / (jnp.sqrt(square_total) + epsilon)
    rms = jnp.sqrt(square_total * (1.0 / (F * R)))
    for low, (i, j) in enumerate(PAIRS):
        block = full[low * BLOCK : (low + 1) * BLOCK] * inverse * inverse
        gram[i * BLOCK : (i + 1) * BLOCK, j * BLOCK : (j + 1) * BLOCK] = block
        if i != j:
            gram[j * BLOCK : (j + 1) * BLOCK, i * BLOCK : (i + 1) * BLOCK] = block.T
    ortho[...] = ortho[...] * inverse

    def step(count, k, carry):
        now = halves(gram[...], count)
        square = mirrored(now[:2], now[:2])
        row_ids = lax.broadcasted_iota(jnp.int32, (R, R), 0)
        col_ids = lax.broadcasted_iota(jnp.int32, (R, R), 1)
        factor = halves(
            jnp.where(row_ids == col_ids, coef_one, 0.0) + coef_two * gram[...] + coef_three * square,
            count,
        )
        ortho[...] = split_product(halves(ortho[...], 2), factor[:2])
        once = halves(mirrored(now, factor), count)
        gram[...] = mirrored(once, factor)
        return carry

    lax.fori_loop(0, FINE, functools.partial(step, 3), 0)
    lax.fori_loop(FINE, ITERS - 1, functools.partial(step, 2), 0)
    now = halves(gram[...], 2)
    first = ortho[...]
    second = split_product(halves(first, 2), now)
    third = split_product(halves(second, 2), now)
    last = coef_one * first + coef_two * second + coef_three * third

    update = last * (0.2 * float(max(F, R)) ** 0.5)
    stepped = weight_in[...] * (1.0 - learn_rate * decay_rate) - learn_rate * update
    master = stepped * scale_out[0:1, 0:1]
    master_out[...] = master
    stores.append(pltpu.make_async_copy(master_out, new_master, s_local.at[6]))
    rounded[...] = master.astype(jnp.bfloat16)

    stores.append(pltpu.make_async_copy(rounded, new_weight.at[z, x], s_local.at[7]))
    bx, az, ax, bz = [], {}, {}, {}
    for r in (1, 3, 2):
        bx.append(
            send(
                rounded.at[CUT:BLOCK],
                new_weight.at[z, x, CUT:BLOCK],
                s_bx.at[r - 1],
                r_bx.at[r - 1],
                at_x((x + r) % NX),
            )
        )

    def first_a(distance):
        for way, to in ((0, (z + distance) % NZ), (1, (z + NZ - distance) % NZ)):
            az[way, distance] = send(
                rounded.at[0:CUT],
                new_weight.at[z, x, 0:CUT],
                s_az.at[way, distance - 1],
                r_az.at[way, distance - 1],
                at_z(to),
            )

    def ring_a(distance):
        for way, zz, to in (
            (0, (z + NZ - distance + 1) % NZ, zup),
            (1, (z + distance - 1) % NZ, zdn),
        ):
            lo, hi = (0, CUT) if distance < 4 else ((0, 48) if way == 0 else (48, CUT))
            piece = new_weight.at[zz, x, lo:hi]
            az[way, distance] = send(
                piece, piece, s_az.at[way, distance - 1], r_az.at[way, distance - 1], at_z(to)
            )

    def ring_b(step, r):
        xx = (x + r) % NX
        for way, zz, to in ((0, (z + NZ - step) % NZ, zup), (1, (z + step) % NZ, zdn)):
            if step > 0:
                bz[way, step - 1, r].wait_recv()
            if step == 3 and (r < 2) != (way == 0):
                continue
            piece = new_weight.at[zz, xx, CUT:BLOCK]
            src = rounded.at[CUT:BLOCK] if step == 0 and r == 0 else piece
            bz[way, step, r] = send(
                src, piece, s_bz.at[way, step, r], r_bz.at[way, step, r], at_z(to)
            )

    def spread(slot, zz, src):
        ax[slot] = [
            send(src, new_weight.at[zz, x, 0:CUT], s_ax.at[slot, 0], r_ax.at[slot, 0], at_x(xr)),
            send(src, new_weight.at[zz, x, 0:CUT], s_ax.at[slot, 1], r_ax.at[slot, 1], at_x(xl)),
        ]

    def spread_on(slot, zz):
        ax[slot][0].wait_recv()
        left = new_weight.at[zz, xl, 0:48]
        ax[slot].append(send(left, left, s_ax.at[slot, 2], r_ax.at[slot, 2], at_x(xr)))
        ax[slot][1].wait_recv()
        right = new_weight.at[zz, xr, 48:CUT]
        ax[slot].append(send(right, right, s_ax.at[slot, 3], r_ax.at[slot, 3], at_x(xl)))

    first_a(1)
    first_a(2)
    spread(0, z, rounded.at[0:CUT])
    ring_b(0, 0)
    stores[1].start()
    stores[2].start()
    drain(sent[:])
    blend_rms[0] = rms[0, 0]
    places = [z]
    for k in range(1, 4):
        places.extend([(z + NZ - k) % NZ, (z + k) % NZ])
    places.append((z + 4) % NZ)

    def arrived(distance):
        az[0, distance].wait_recv()
        az[1, distance].wait_recv()

    def spread_two(k):
        for slot in (2 * k - 1, 2 * k):
            spread(slot, places[slot], new_weight.at[places[slot], x, 0:CUT])

    arrived(1)
    spread_two(1)
    arrived(2)
    ring_a(3)
    spread_two(2)
    for r in (1, 3, 2):
        bx[(3, 1, 2).index(r)].wait_recv()
        ring_b(0, r)
    spread_on(0, z)
    ring_b(1, 0)
    arrived(3)
    ring_a(4)
    spread_two(3)
    spread_on(1, places[1])
    spread_on(2, places[2])
    for r in (1, 3, 2):
        ring_b(1, r)
    arrived(4)
    spread(7, places[7], new_weight.at[places[7], x, 0:CUT])
    spread_on(3, places[3])
    spread_on(4, places[4])
    for r in (0, 1, 3, 2):
        ring_b(2, r)
    spread_on(5, places[5])
    spread_on(6, places[6])
    for r in (0, 1, 3, 2):
        ring_b(3, r)
    spread_on(7, places[7])
    for r in range(4):
        bz[r // 2, 3, r].wait_recv()
    stores[2].wait()
    for slot in range(8):
        ax[slot][2].wait_recv()
        ax[slot][3].wait_recv()
    for copies in (bx, az.values(), bz.values(), *ax.values()):
        for copy in copies:
            copy.wait_send()
    stores[0].wait()
    stores[1].wait()


def local(grads, momentum, weight, max_logits, threshold):
    smem = pl.BlockSpec(memory_space=pltpu.SMEM)
    hbm = pl.BlockSpec(memory_space=pl.ANY)
    f32, bf16, i32 = jnp.float32, jnp.bfloat16, jnp.int32
    dma = pltpu.SemaphoreType.DMA
    new_master, new_momentum, new_weight, blend_rms = pl.pallas_call(
        kernel,
        out_shape=(
            jax.ShapeDtypeStruct((BLOCK, R), f32),
            jax.ShapeDtypeStruct((BLOCK, R), f32),
            jax.ShapeDtypeStruct((NZ, NX, BLOCK, R), bf16),
            jax.ShapeDtypeStruct((1,), f32),
        ),
        in_specs=[hbm, hbm, hbm, hbm, smem],
        out_specs=(hbm, hbm, hbm, smem),
        scratch_shapes=[
            pltpu.VMEM((NZ, BLOCK, CA), bf16),
            pltpu.VMEM((NZ, NX, BLOCK, CB), bf16),
            pltpu.VMEM((8, 3, BLOCK, CA), bf16),
            pltpu.VMEM((2, 4, BLOCK, CA), f32),
            pltpu.VMEM((2, 4, BLOCK, CA), f32),
            pltpu.VMEM((2, 4, NX, BLOCK, CB), f32),
            pltpu.VMEM((2, 4, NX, BLOCK, CB), f32),
            pltpu.VMEM((2, 2, BLOCK, CB), bf16),
            pltpu.VMEM((NX, BLOCK, CB), f32),
            pltpu.VMEM((3, BLOCK, CB), f32),
            pltpu.VMEM((BLOCK, R), f32),
            pltpu.VMEM((BLOCK, R), f32),
            pltpu.VMEM((BLOCK, R), f32),
            pltpu.VMEM((BLOCK, R), f32),
            pltpu.VMEM((1, LAYERS, HEADS), i32),
            pltpu.VMEM((2 * HALF, BLOCK), f32),
            pltpu.VMEM((HALF, BLOCK), f32),
            pltpu.VMEM((HALF, BLOCK), f32),
            pltpu.VMEM((15, PART, BLOCK), f32),
            pltpu.VMEM((PART, BLOCK), f32),
            pltpu.VMEM((4, PART, BLOCK), f32),
            pltpu.VMEM((2 * HALF, BLOCK), f32),
            pltpu.VMEM((R, R), f32),
            pltpu.VMEM((BLOCK, R), f32),
            pltpu.VMEM((BLOCK, R), bf16),
            pltpu.VMEM((8, 128), i32),
            pltpu.VMEM((3, 8, 128), i32),
            pltpu.VMEM((8, 128), i32),
            pltpu.VMEM((8, 128), i32),
            pltpu.VMEM((8, 128), f32),
            pltpu.VMEM((4, 8, 128), i32),
            pltpu.SemaphoreType.REGULAR,
            dma((8,)),
            dma((8, 3)),
            dma((8, 3)),
            dma((2, 4)),
            dma((2, 4)),
            dma((3, 4)),
            dma((3, 4)),
            dma((10,)),
            dma((10,)),
            dma((50,)),
            dma((50,)),
            dma((2, 4)),
            dma((2, 4)),
            dma((8, 4)),
            dma((8, 4)),
            dma((3,)),
            dma((3,)),
            dma((2, 4, 4)),
            dma((2, 4, 4)),
        ],
        compiler_params=pltpu.CompilerParams(
            collective_id=0, has_side_effects=True, vmem_limit_bytes=48 * 1024 * 1024
        ),
        name="muon",
    )(grads.reshape(NZ, NX, BLOCK, R), momentum, weight, max_logits, threshold)
    return (new_master, new_momentum, new_weight.reshape(NZ * NX * BLOCK, R), blend_rms)


def solution(mesh):
    return jax.shard_map(
        local,
        mesh=mesh,
        in_specs=(
            P("dp", "col", None),
            P(("col", "dp"), None),
            P(("col", "dp"), None),
            P("dp", None, None),
            P(),
        ),
        out_specs=(P(("col", "dp"), None), P(("col", "dp"), None), P("col", None), P("col")),
        check_vma=False,
    )
```
